32 devices in a mesh: mode: 8 (over y, x, core), elem: 4 (over z).
Axes of the slice: x: 2, y: 2, z: 4, core: 2. Of those that a mesh axis runs over, the one named last changes fastest.
Arguments:
- velocity: float32 [3, 128, 4096], P(None, 'mode', 'elem'), may hold values from -1.5 to 1.5
- metric_main: float32 [2, 4096], P(None, 'elem'), may hold values from 0.5 to 1.5
- metric_cross: float32 [2, 4096], P(None, 'elem'), may hold values from -0.5 to 0.5
- stiffness: float32 [4096, 512], P('elem'), as said below
- mass: float32 [4096], P('elem'), may hold values from 0.5 to 2
- precond: float32 [64, 4096, 512], P('mode', 'elem'), as said below
- trace_map: int32 [8, 2, 32], P('elem'), may hold values from 0 to 511, as said below
Outputs:
- new_velocity: float32 [3, 128, 4096], P(None, 'mode', 'elem')
The draws below stay inside these ranges and needn't reach their ends.
Inputs may be any that keep to these rules, and one draw needn't show every extreme that they name: trace_map[q, 0] and trace_map[q, 1] together hold 64 distinct points of patch q; slot j of trace_map[q, 1] and slot j of trace_map[q + 1, 0] are the same plane point. `stiffness`: each 512 x 512 block is symmetric. `precond`: one 512 x 512 matrix for each mode and patch.
All inputs are finite; a program needn't handle non-finite values.
Results may differ from the reference program's by a relative error of at most 0.0003.
Values sent between devices are 32-bit elements; how exact they have to be, the bound alone decides.
A program may use at most 128 MiB of HBM per device.

```python
import math
import jax
import jax.numpy as jnp
import numpy as np
from jax import lax

MODES = 64
KZ = 128
NZ = 256
L = 512
TRACE = 32
NPATCH = 8
NPTS = 4096
STEPS = 4
ITERS = 4


def draw_stiffness(key, part):
    noise = jax.random.normal(jax.random.fold_in(key, 31), (NPATCH, L, L), jnp.float32)
    symmetric = (noise + jnp.swapaxes(noise, 1, 2)) * (0.5 / math.sqrt(2.0 * L))
    diagonal = jax.random.uniform(jax.random.fold_in(key, 32), (NPATCH, L, 1), jnp.float32, 1.0, 3.0)
    row_numbers = lax.broadcasted_iota(jnp.int32, (L, L), 0)
    column_numbers = lax.broadcasted_iota(jnp.int32, (L, L), 1)
    identity = (row_numbers == column_numbers).astype(jnp.float32)[None]
    blocks = symmetric * (1.0 - identity) + identity * diagonal
    return blocks.reshape(NPATCH * L, L)


def draw_precond(key, part):
    noise = jax.random.normal(jax.random.fold_in(key, 41), (MODES, NPATCH * L, L), jnp.float32)
    diagonal = jax.random.uniform(jax.random.fold_in(key, 42), (MODES, NPATCH * L, 1), jnp.float32, 0.8, 1.2)
    row_numbers = lax.broadcasted_iota(jnp.int32, (NPATCH * L, L), 0) % L
    column_numbers = lax.broadcasted_iota(jnp.int32, (NPATCH * L, L), 1)
    identity = (row_numbers == column_numbers).astype(jnp.float32)[None]
    wavenumber = 4.0 * jnp.arange(MODES, dtype=jnp.float32) / MODES
    mode_scale = 1.0 / (2.0 + 0.5 * wavenumber * wavenumber)
    return (identity * diagonal + 0.3 / math.sqrt(L) * noise) * mode_scale[:, None, None]


def draw_trace_map(key, part):
    patch_keys = jax.random.split(jax.random.fold_in(key, 51), NPATCH)
    scores = jax.vmap(lambda patch_key: jax.random.permutation(patch_key, L))(patch_keys).astype(jnp.int32)
    first_patch = (jnp.arange(NPATCH, dtype=jnp.int32) == 0)[:, None]
    position = jnp.arange(L, dtype=jnp.int32)[None, :]
    scores = jnp.where(first_patch & (position == L - 1), -2, scores)
    scores = jnp.where(first_patch & (position == 0), -1, scores)
    ordering = jnp.argsort(scores, axis=1, stable=True).astype(jnp.int32)
    return ordering[:, :2 * TRACE].reshape(NPATCH, 2, TRACE)


def level_of(own_key, extent, pieces, smallest, high):
    def one(dim, shards_of):
        heights = jax.random.uniform(jax.random.fold_in(jax.random.fold_in(own_key, 6), dim), (shards_of,), jnp.float32, smallest / len(pieces), high / len(pieces))
        return jnp.repeat(jnp.exp(heights), extent[dim] // shards_of).reshape((-1,) + (1,) * (len(extent) - dim - 1))

    gain = one(*pieces[0])
    for cut in pieces[1:]:
        gain = gain * one(*cut)
    return gain


def bell_draw(key, dims, scale, most, cuts=(), kind=jnp.bfloat16):
    array = scale * jax.random.normal(key, dims, jnp.float32)
    if cuts:
        array = array * level_of(key, dims, cuts, -0.22, 0.18)
    return jnp.clip(array, -most, most).astype(kind)


def setup_inputs(seed: int = 0) -> dict:
    key_list = jax.random.split(jax.random.key(seed), 8)
    velocity = bell_draw(key_list[0], (3, KZ, NPTS), 0.25, 1.5, ((1, 8), (2, 4)), jnp.float32)
    metric_main = jnp.clip(0.5 + 1.0 * jax.random.uniform(key_list[1], (2, NPTS), jnp.float32) ** level_of(key_list[1], (2, NPTS), ((1, 4),), -0.2, 0.2), 0.5, 1.5)
    metric_cross = jnp.clip(jax.random.uniform(key_list[2], (2, NPTS), jnp.float32, -0.5, 0.5) * level_of(key_list[2], (2, NPTS), ((1, 4),), -0.4, 0.0), -0.5, 0.5)
    stiffness = draw_stiffness(jax.random.fold_in(key_list[7], 71), 0)
    mass = jnp.clip(jnp.exp(math.log(2.0) - 1.3862944 * jax.random.uniform(key_list[4], (NPATCH * L,), jnp.float32) ** level_of(key_list[4], (NPATCH * L,), ((0, 4),), -0.2, 0.2)), 0.5, 2.0)
    precond = draw_precond(jax.random.fold_in(key_list[7], 71), 0)
    trace_map = draw_trace_map(jax.random.fold_in(key_list[7], 71), 0)
    return {"velocity": velocity, "metric_main": metric_main, "metric_cross": metric_cross, "stiffness": stiffness, "mass": mass, "precond": precond, "trace_map": trace_map}


highest_precision = lax.Precision.HIGHEST
viscous_step = 0.5
time_step = 0.02
relaxation = 0.8


def chebyshev_matrix():
    node_points = np.cos(np.pi * np.arange(8) / 7.0)
    weights = np.where((np.arange(8) == 0) | (np.arange(8) == 7), 2.0, 1.0)
    parity = np.where((np.arange(8)[:, None] + np.arange(8)[None, :]) % 2 == 0, 1.0, -1.0)
    identity = np.eye(8)
    spacing = node_points[:, None] - node_points[None, :] + identity
    off_diagonal = (weights[:, None] / weights[None, :]) * parity / spacing * (1.0 - identity)
    return off_diagonal - identity * off_diagonal.sum(axis=1)[:, None]


def spanwise_tables():
    spanwise = jnp.arange(NZ, dtype=jnp.int32)
    row_numbers = jnp.arange(KZ, dtype=jnp.int32)
    wavenumber = row_numbers // 2
    product = (spanwise[:, None] * wavenumber[None, :]) % NZ
    phase_angle = (2.0 * math.pi / NZ) * product.astype(jnp.float32)
    is_sine = (row_numbers % 2 == 1)[None, :]
    basis_table = jnp.where(is_sine, jnp.sin(phase_angle), jnp.cos(phase_angle))
    wave_rate = 4.0 * wavenumber.astype(jnp.float32) / MODES
    slope_table = jnp.where(is_sine, wave_rate[None, :] * jnp.cos(phase_angle), -wave_rate[None, :] * jnp.sin(phase_angle))
    norm_factor = jnp.where(row_numbers == 0, 1.0 / NZ, 2.0 / NZ).astype(jnp.float32)
    forward = basis_table.T * norm_factor[:, None]
    return basis_table, slope_table, forward, wave_rate


def reference(velocity, metric_main, metric_cross, stiffness, mass, precond, trace_map):
    chebyshev = jnp.asarray(chebyshev_matrix(), jnp.float32)
    basis_table, slope_table, forward, wave_rate = spanwise_tables()
    wave_modes = wave_rate.reshape(MODES, 2)[:, 0]
    damping = (1.0 + viscous_step * wave_rate * wave_rate)[None, :, None, None]
    patches = stiffness.reshape(NPATCH, L, L)
    patch_mass = mass.reshape(NPATCH, L)
    inverse = precond.reshape(MODES, NPATCH, L, L)
    left_trace = trace_map[:, 0]
    right_trace = trace_map[:, 1]
    patch_rows = jnp.arange(NPATCH)[:, None]
    patch_numbers = jnp.arange(NPATCH)
    left_gain = jnp.broadcast_to((patch_numbers > 0)[:, None], left_trace.shape).astype(jnp.float32)
    right_gain = jnp.broadcast_to((patch_numbers < NPATCH - 1)[:, None], right_trace.shape).astype(jnp.float32)
    multiplicity = jnp.ones((NPATCH, L), jnp.float32).at[patch_rows, left_trace].add(left_gain).at[patch_rows, right_trace].add(right_gain)
    weight = relaxation / (multiplicity * multiplicity)

    def assemble(values):
        left_values = values[:, :, patch_rows, left_trace]
        right_values = values[:, :, patch_rows, right_trace]
        nothing = jnp.zeros_like(left_values[:, :, :1])
        from_below = jnp.concatenate([nothing, right_values[:, :, :-1]], axis=2)
        from_above = jnp.concatenate([left_values[:, :, 1:], nothing], axis=2)
        return values.at[:, :, patch_rows, left_trace].add(from_below).at[:, :, patch_rows, right_trace].add(from_above)

    state = velocity
    for time_level in range(STEPS):
        element_view = state.reshape(3, KZ, NPTS // 64, 8, 8)
        xi_slope = jnp.einsum("creyj,xj->creyx", element_view, chebyshev, precision=highest_precision).reshape(state.shape)
        eta_slope = jnp.einsum("crejx,yj->creyx", element_view, chebyshev, precision=highest_precision).reshape(state.shape)
        grad_x = metric_main[0] * xi_slope + metric_cross[0] * eta_slope
        grad_y = metric_cross[1] * xi_slope + metric_main[1] * eta_slope
        pairs = state.reshape(3, MODES, 2, NPTS)
        grad_z = jnp.stack([wave_modes[None, :, None] * pairs[:, :, 1], -wave_modes[None, :, None] * pairs[:, :, 0]], axis=2).reshape(state.shape)
        fields = jnp.concatenate([state, grad_x, grad_y, grad_z], axis=0)
        physical = jnp.einsum("frp,zr->fpz", fields, basis_table, precision=highest_precision)
        advection = physical[0:1] * physical[3:6] + physical[1:2] * physical[6:9] + physical[2:3] * physical[9:12]
        advection_hat = jnp.einsum("ipz,rz->irp", advection, forward, precision=highest_precision)
        source = (state - time_step * advection_hat).reshape(3, KZ, NPATCH, L)
        local_term = patch_mass * source
        iterate = jnp.zeros_like(source)
        for sweep_number in range(ITERS):
            if sweep_number == 0:
                residual = assemble(local_term)
            else:
                stiff_part = jnp.einsum("pij,crpj->crpi", patches, iterate, precision=highest_precision)
                residual = assemble(local_term - viscous_step * stiff_part - damping * patch_mass * iterate)
            grouped = residual.reshape(3, MODES, 2, NPATCH, L)
            correction = jnp.einsum("kpij,ckhpj->ckhpi", inverse, grouped, precision=highest_precision).reshape(3, KZ, NPATCH, L)
            iterate = iterate + weight * assemble(correction)
        state = iterate.reshape(3, KZ, NPTS)
    return state
```

```python
import functools
import math

import jax
import jax.numpy as jnp
import numpy as np
from jax import lax
from jax.experimental import pallas as pl
from jax.experimental.pallas import tpu as pltpu
from jax.sharding import PartitionSpec as P

NZ = 256
STEPS = 4
ITERS = 4
LANES = 128

viscous_step = 0.5
time_step = 0.02
relaxation = 0.8
f32 = jnp.float32
bf16 = jnp.bfloat16
MODES = 64
KZ = 128
highest_precision = lax.Precision.HIGHEST


def chebyshev_matrix():
    node_points = np.cos(np.pi * np.arange(8) / 7.0)
    weights = np.where((np.arange(8) == 0) | (np.arange(8) == 7), 2.0, 1.0)
    parity = np.where((np.arange(8)[:, None] + np.arange(8)[None, :]) % 2 == 0, 1.0, -1.0)
    identity = np.eye(8)
    spacing = node_points[:, None] - node_points[None, :] + identity
    off_diagonal = weights[:, None] / weights[None, :] * parity / spacing * (1.0 - identity)
    return off_diagonal - identity * off_diagonal.sum(axis=1)[:, None]


def pair(table):
    table = np.asarray(table, np.float32)
    high = table.astype(bf16)
    low = (table - high.astype(np.float32)).astype(bf16)
    return high, low


def spanwise_tables(modes):
    angle = 2.0 * math.pi / NZ * (np.arange(NZ)[:, None] * np.arange(modes)[None, :] % NZ)
    rate = 4.0 * np.arange(modes) / modes
    cosine, sine = np.cos(angle), np.sin(angle)
    basis = np.concatenate([cosine, sine], axis=1)
    slope = np.concatenate([-rate * sine, rate * cosine], axis=1)
    factor = np.full(2 * modes, 2.0 / NZ)
    factor[0] = 1.0 / NZ
    forward = basis.T * factor[:, None]

    def left_three(table):
        high, low = pair(table)
        return np.concatenate([high, low, high], axis=1)

    return left_three(basis), left_three(slope), np.stack(pair(forward))


def plane_tables():
    chebyshev = chebyshev_matrix()
    position = np.arange(LANES)
    column, row, element = position % 8, position // 8 % 8, position // 64
    same = element[:, None] == element[None, :]
    xi = np.where(same & (row[:, None] == row[None, :]), chebyshev.T[column][:, column], 0.0)
    eta = np.where(same & (column[:, None] == column[None, :]), chebyshev.T[row][:, row], 0.0)
    return np.stack(pair(np.concatenate([xi, eta], axis=1)))


def row_order(modes):
    move = np.zeros((modes * 16, 2 * 6 * modes), np.float32)
    for part in range(2):
        for field in range(6):
            for mode in range(modes):
                move[mode * 16 + part * 8 + field, (part * 6 + field) * modes + mode] = 1.0
    back = move[:, : 6 * modes] + move[:, 6 * modes :]
    return move.astype(bf16), back.T.astype(bf16)


def dot(a, b):
    return lax.dot_general(a, b, (((1,), (0,)), ((), ())), preferred_element_type=f32)


def split(value):
    high = value.astype(bf16)
    return high, (value - high.astype(f32)).astype(bf16)


def stacked(value):
    return jnp.concatenate(split(value), axis=0)


def folded(value):
    half = value.shape[0] // 2
    return value[:half] + value[half:]


def product(value, high, low):
    both = stacked(value)
    return folded(dot(both, high)) + dot(both[: value.shape[0]], low)


def moved(value, one_hot):
    return folded(dot(stacked(value), one_hot))


def kernel(
    ranks,
    depth,
    modes,
    patches,
    width,
    trace,
    share,
    velocity,
    metrics,
    stiffness,
    mass,
    weight,
    pick,
    pick_back,
    basis,
    slope,
    forward,
    plane,
    move,
    back,
    precond,
    out,
    raw,
    inverse_high,
    inverse_low,
    stiff_high,
    stiff_low,
    across,
    edge_high,
    edge_low,
    corner_out,
    corner_in,
    corner_high,
    corner_low,
    state,
    coef,
    hat,
    returned,
    local,
    damped,
    residual,
    correction,
    note_out,
    note_in,
    raw_sem,
    own_sem,
    send_sem,
    coef_sem,
    hat_sem,
    note_send,
    note_recv,
    corner_send,
    corner_recv,
):
    me = lax.axis_index("mode")
    place = lax.axis_index("elem")
    has = (place > 0, place < depth - 1)
    beside = (place - 1, place + 1)
    rows = 6 * modes

    def patch_of(p):
        return pl.ds(p * width, width)

    for k in range(modes):
        for p in range(patches):
            pltpu.make_async_copy(
                precond.at[k, patch_of(p), :], raw.at[k, patch_of(p), :], raw_sem.at[k, p]
            ).start()

    note_in[...] = jnp.zeros_like(note_in)
    corner_in[...] = jnp.zeros_like(corner_in)
    state[...] = velocity[...]

    barrier = pltpu.get_barrier_semaphore()
    for offset in range(1, ranks):
        pl.semaphore_signal(
            barrier, 1, device_id={"mode": lax.rem(me + offset, ranks)},
            device_id_type=pl.DeviceIdType.MESH,
        )
    for side in range(2):
        @pl.when(has[side])
        def _():
            pl.semaphore_signal(
                barrier, 1, device_id={"elem": beside[side]}, device_id_type=pl.DeviceIdType.MESH
            )
    neighbours = jnp.minimum(place, 1) + jnp.minimum(depth - 1 - place, 1)
    pl.semaphore_wait(barrier, ranks - 1 + neighbours)

    def points_of(rank):
        return pl.ds(pl.multiple_of(rank * share, share), share)

    def modes_of(rank):
        return pl.ds(pl.multiple_of(rank * modes, modes), modes)

    def coef_copy(offset):
        to = lax.rem(me + offset, ranks)
        return pltpu.make_async_remote_copy(
            src_ref=state.at[:, :, points_of(to)],
            dst_ref=coef.at[:, modes_of(me), :],
            send_sem=send_sem.at[0, offset],
            recv_sem=coef_sem.at[offset],
            device_id={"mode": to},
            device_id_type=pl.DeviceIdType.MESH,
        )

    def hat_copy(offset):
        to = lax.rem(me + offset, ranks)
        return pltpu.make_async_remote_copy(
            src_ref=hat.at[:, modes_of(to), :],
            dst_ref=returned.at[:, :, points_of(me)],
            send_sem=send_sem.at[1, offset],
            recv_sem=hat_sem.at[offset],
            device_id={"mode": to},
            device_id_type=pl.DeviceIdType.MESH,
        )

    def own_coef():
        return pltpu.make_async_copy(
            state.at[:, :, points_of(me)], coef.at[:, modes_of(me), :], own_sem.at[0]
        )

    def own_hat():
        return pltpu.make_async_copy(
            hat.at[:, modes_of(me), :], returned.at[:, :, points_of(me)], own_sem.at[1]
        )

    def send_coef():
        for offset in range(1, ranks):
            coef_copy(offset).start()
        own_coef().start()

    def note_copy(side, slot):
        return pltpu.make_async_remote_copy(
            src_ref=note_out.at[side],
            dst_ref=note_in.at[slot, 1 - side],
            send_sem=note_send.at[side],
            recv_sem=note_recv.at[slot, 1 - side],
            device_id={"elem": beside[side]},
            device_id_type=pl.DeviceIdType.MESH,
        )

    def corner_copy(side):
        return pltpu.make_async_remote_copy(
            src_ref=corner_out.at[side],
            dst_ref=corner_in.at[1 - side],
            send_sem=corner_send.at[side],
            recv_sem=corner_recv.at[1 - side],
            device_id={"elem": beside[side]},
            device_id_type=pl.DeviceIdType.MESH,
        )

    def note_wait(side, slot):
        note_copy(side, slot).wait_send()
        pltpu.make_async_remote_copy(
            src_ref=note_out.at[side],
            dst_ref=note_in.at[slot, side],
            send_sem=note_send.at[side],
            recv_sem=note_recv.at[slot, side],
            device_id={"elem": beside[side]},
            device_id_type=pl.DeviceIdType.MESH,
        ).wait_recv()

    def corner_wait(side):
        corner_copy(side).wait_send()
        pltpu.make_async_remote_copy(
            src_ref=corner_out.at[side],
            dst_ref=corner_in.at[side],
            send_sem=corner_send.at[side],
            recv_sem=corner_recv.at[side],
            device_id={"elem": beside[side]},
            device_id_type=pl.DeviceIdType.MESH,
        ).wait_recv()

    send_coef()

    for p in range(patches):
        stiff_high[p], stiff_low[p] = split(viscous_step * stiffness[patch_of(p), :])
    for p in range(patches - 1):
        across[p, 0] = dot(pick[p, 1, 0], pick_back[p + 1, 0, 0]).astype(bf16)
        across[p, 1] = dot(pick[p + 1, 0, 0], pick_back[p, 1, 0]).astype(bf16)
    number = lax.broadcasted_iota(jnp.int32, (rows, 1), 0) % modes + me * modes
    rate = 4.0 * number.astype(f32) / (modes * ranks)
    damped[...] = (1.0 + viscous_step * rate * rate) * mass[...]
    edge_patch = (0, patches - 1)

    def prepare(k, carry):
        for p in range(patches):
            pltpu.make_async_copy(
                precond.at[k, patch_of(p), :], raw.at[k, patch_of(p), :], raw_sem.at[k, p]
            ).wait()
            high, low = split(raw[k, patch_of(p), :].T)
            inverse_high[k, p] = high
            inverse_low[k, p] = low
        for side in range(2):
            p = edge_patch[side]
            span = pl.ds(pl.multiple_of(k * trace, trace), trace)
            choose = pick_back[p, side, 0][:trace]
            edge_high[side, span, :] = dot(choose, inverse_high[k, p]).astype(bf16)
            edge_low[side, span, :] = dot(choose, inverse_low[k, p]).astype(bf16)
        return carry

    lax.fori_loop(0, modes, prepare, 0)
    for side in range(2):
        choose = pick[edge_patch[side], side, 1]
        corner_out[side] = dot(edge_high[side], choose) + dot(edge_low[side], choose)

        @pl.when(has[side])
        def _():
            corner_copy(side).start()
    for side in range(2):
        @pl.when(has[side])
        def _():
            corner_wait(side)
        corner_high[side], corner_low[side] = split(corner_in[side])

    lane = lax.broadcasted_iota(jnp.int32, (rows, LANES), 1)
    wide = modes * trace
    block_mask = (
        lax.broadcasted_iota(jnp.int32, (rows, wide), 0) % modes
        == lax.broadcasted_iota(jnp.int32, (rows, wide), 1) // trace
    )

    def spread(note):
        first = jnp.where(lane < trace, note, 0.0)
        total = first
        for turn in range(1, LANES // trace):
            total = total + pltpu.roll(first, turn * trace, 1)
        tiled = jnp.concatenate([total] * (wide // LANES), axis=1)
        return jnp.where(block_mask, tiled, 0.0)

    def advect():
        for offset in range(1, ranks):
            coef_copy(offset).wait_recv()
        own_coef().wait()
        fields = coef[...].reshape(6 * modes * ranks, share)
        high, low = split(fields)
        slopes = dot(high, plane[0]) + dot(low, plane[0]) + dot(high, plane[1])
        xi, eta = slopes[:, :share], slopes[:, share:]
        grad_x = metrics[0:1] * xi + metrics[2:3] * eta
        grad_y = metrics[3:4] * xi + metrics[1:2] * eta
        each = 2 * modes * ranks

        def physical(table, value, c):
            high, low = split(value[c * each : (c + 1) * each])
            return dot(table, jnp.concatenate([high, high, low], axis=0))

        u, v, w = (physical(basis[...], fields, c) for c in range(3))
        for c in range(3):
            advection = (
                u * physical(basis[...], grad_x, c)
                + v * physical(basis[...], grad_y, c)
                + w * physical(slope[...], fields, c)
            )
            high, low = split(advection)
            total = dot(forward[0], high) + dot(forward[0], low) + dot(forward[1], high)
            hat[pl.ds(2 * c, 2)] = total.reshape(2, modes * ranks, share)
        for offset in range(1, ranks):
            hat_copy(offset).start()
        own_hat().start()
        for offset in range(1, ranks):
            hat_copy(offset).wait_recv()
        own_hat().wait()
        for offset in range(1, ranks):
            coef_copy(offset).wait_send()
            hat_copy(offset).wait_send()
        source = state[...] - time_step * returned[...]
        local[...] = mass[...] * source.reshape(rows, patches * width)
        state[...] = jnp.zeros_like(state)

    def assembled(parts):
        result = list(parts)
        for p in range(patches - 1):
            result[p + 1] = result[p + 1] + moved(parts[p], across[p, 0])
            result[p] = result[p] + moved(parts[p + 1], across[p, 1])
        return result

    def sweep(number, carry):
        slot = lax.rem(number, 2)
        terms = []
        for p in range(patches):
            value = state[:, :, patch_of(p)].reshape(rows, width)
            terms.append(
                local[:, patch_of(p)]
                - product(value, stiff_high[p], stiff_low[p])
                - damped[:, patch_of(p)] * value
            )
        terms = assembled(terms)
        parts = []
        for p in range(patches):
            ordered = dot(move[...], stacked(terms[p])).astype(bf16)
            found = []
            for k in range(modes):
                line = ordered[k * 16 : (k + 1) * 16]
                found.append(dot(line, inverse_high[k, p]) + dot(line, inverse_low[k, p]))
            high, low = split(jnp.concatenate(found, axis=0))
            parts.append(dot(back[...], high) + dot(back[...], low))
        notes = []
        for side in range(2):
            p = edge_patch[side]
            note = folded(
                dot(stacked(terms[p]), pick[p, side, 0]) + dot(stacked(parts[p]), pick[p, side, 1])
            )
            note_out[side] = note
            notes.append(note)

            @pl.when(has[side])
            def _():
                note_copy(side, slot).start()
        near = [product(spread(notes[side]), corner_high[side], corner_low[side]) for side in range(2)]
        for side in range(2):
            @pl.when(has[side])
            def _():
                note_wait(side, slot)
        gains = []
        for side in range(2):
            p = edge_patch[side]
            note = note_in[slot, side]
            parts[p] = parts[p] + product(spread(note), edge_high[side], edge_low[side])
            gains.append(moved(note + near[side], pick_back[p, side, 1]))
        total = assembled(parts)
        for side in range(2):
            p = edge_patch[side]
            total[p] = total[p] + gains[side]
        for p in range(patches):
            step = weight[:, patch_of(p)] * total[p]
            state[:, :, patch_of(p)] = state[:, :, patch_of(p)] + step.reshape(6, modes, width)
        return carry

    def level(number, carry):
        advect()
        lax.fori_loop(0, ITERS, sweep, 0)

        @pl.when(number < STEPS - 1)
        def _():
            send_coef()

        return carry

    lax.fori_loop(0, STEPS, level, 0)
    out[...] = state[...]


def on_device(velocity, metric_main, metric_cross, stiffness, mass, precond, trace_map):
    ranks, depth = lax.axis_size("mode"), lax.axis_size("elem")
    rows, points = velocity.shape[1:]
    modes = rows // 2
    patches, _, trace = trace_map.shape
    width = stiffness.shape[1]
    share = points // ranks
    if modes % 8 or share != LANES or LANES % trace or (modes * trace) % LANES or patches < 2:
        return general_device(
            velocity, metric_main, metric_cross, stiffness, mass, precond, trace_map
        )
    start = lax.axis_index("mode") * share
    metrics = lax.dynamic_slice_in_dim(
        jnp.concatenate([metric_main, metric_cross], axis=0), start, share, 1
    )
    numbers = jnp.arange(width, dtype=jnp.int32)
    slots = jnp.stack(
        [
            jnp.pad(trace_map, ((0, 0), (0, 0), (0, LANES - trace)), constant_values=-1),
            jnp.pad(trace_map, ((0, 0), (0, 0), (trace, LANES - 2 * trace)), constant_values=-1),
        ],
        axis=2,
    )
    pick = (slots[:, :, :, None, :] == numbers[:, None]).astype(bf16)
    pick_back = (slots[:, :, :, :, None] == numbers).astype(bf16)
    global_patch = lax.axis_index("elem") * patches + jnp.arange(patches)
    gains = jnp.stack([global_patch > 0, global_patch < patches * depth - 1], axis=1)
    hits = (trace_map[:, :, :, None] == numbers) & gains[:, :, None, None]
    multiplicity = 1.0 + jnp.sum(hits.astype(f32), axis=(1, 2))
    weight = (relaxation / (multiplicity * multiplicity)).reshape(1, points)
    basis, slope, forward = spanwise_tables(modes * ranks)
    move, back = row_order(modes)
    ordered = velocity.reshape(3, modes, 2, points).swapaxes(1, 2).reshape(6, modes, points)
    vmem = pl.BlockSpec(memory_space=pltpu.VMEM)
    wide = modes * trace
    blocks = (modes, patches, width, width)
    result = pl.pallas_call(
        functools.partial(kernel, ranks, depth, modes, patches, width, trace, share),
        out_shape=jax.ShapeDtypeStruct((6, modes, points), f32),
        in_specs=[vmem] * 13 + [pl.BlockSpec(memory_space=pl.ANY)],
        out_specs=vmem,
        scratch_shapes=[
            pltpu.VMEM((modes, patches * width, width), f32),
            pltpu.VMEM(blocks, bf16),
            pltpu.VMEM(blocks, bf16),
            pltpu.VMEM((patches, width, width), bf16),
            pltpu.VMEM((patches, width, width), bf16),
            pltpu.VMEM((max(patches - 1, 1), 2, width, width), bf16),
            pltpu.VMEM((2, wide, width), bf16),
            pltpu.VMEM((2, wide, width), bf16),
            pltpu.VMEM((2, wide, LANES), f32),
            pltpu.VMEM((2, wide, LANES), f32),
            pltpu.VMEM((2, wide, LANES), bf16),
            pltpu.VMEM((2, wide, LANES), bf16),
            pltpu.VMEM((6, modes, points), f32),
            pltpu.VMEM((6, modes * ranks, share), f32),
            pltpu.VMEM((6, modes * ranks, share), f32),
            pltpu.VMEM((6, modes, points), f32),
            pltpu.VMEM((6 * modes, points), f32),
            pltpu.VMEM((6 * modes, points), f32),
            pltpu.VMEM((6 * modes, points), f32),
            pltpu.VMEM((6 * modes, points), f32),
            pltpu.VMEM((2, 6 * modes, LANES), f32),
            pltpu.VMEM((2, 2, 6 * modes, LANES), f32),
            pltpu.SemaphoreType.DMA((modes, patches)),
            pltpu.SemaphoreType.DMA((2,)),
            pltpu.SemaphoreType.DMA((2, ranks)),
            pltpu.SemaphoreType.DMA((ranks,)),
            pltpu.SemaphoreType.DMA((ranks,)),
            pltpu.SemaphoreType.DMA((2,)),
            pltpu.SemaphoreType.DMA((2, 2)),
            pltpu.SemaphoreType.DMA((2,)),
            pltpu.SemaphoreType.DMA((2,)),
        ],
        compiler_params=pltpu.CompilerParams(
            collective_id=0, has_side_effects=True, vmem_limit_bytes=56 * 1024 * 1024
        ),
    )(
        ordered,
        metrics,
        stiffness,
        mass.reshape(1, points),
        weight,
        pick,
        pick_back,
        jnp.asarray(basis),
        jnp.asarray(slope),
        jnp.asarray(forward),
        jnp.asarray(plane_tables()),
        jnp.asarray(move),
        jnp.asarray(back),
        precond,
    )
    return result.reshape(3, 2, modes, points).swapaxes(1, 2).reshape(3, rows, points)


def shifted(value, axis, steps):
    count = lax.axis_size(axis)
    initial, last = (max(0, -steps), min(count, count - steps))
    return lax.ppermute(value, axis, [(source, source + steps) for source in range(initial, last)])


def general_spanwise():
    spanwise = jnp.arange(NZ, dtype=jnp.int32)
    row_numbers = jnp.arange(KZ, dtype=jnp.int32)
    wavenumber = row_numbers // 2
    product = spanwise[:, None] * wavenumber[None, :] % NZ
    phase_angle = 2.0 * math.pi / NZ * product.astype(jnp.float32)
    is_sine = (row_numbers % 2 == 1)[None, :]
    basis_table = jnp.where(is_sine, jnp.sin(phase_angle), jnp.cos(phase_angle))
    wave_rate = 4.0 * wavenumber.astype(jnp.float32) / MODES
    slope_table = jnp.where(
        is_sine,
        wave_rate[None, :] * jnp.cos(phase_angle),
        -wave_rate[None, :] * jnp.sin(phase_angle),
    )
    norm_factor = jnp.where(row_numbers == 0, 1.0 / NZ, 2.0 / NZ).astype(jnp.float32)
    forward = basis_table.T * norm_factor[:, None]
    return (basis_table, slope_table, forward, wave_rate)


def general_plane(chebyshev):
    position = jnp.arange(128, dtype=jnp.int32)
    node_column = position % 8
    node_row = position // 8 % 8
    element = position // 64
    eight = jnp.arange(8, dtype=jnp.int32)[None, :]
    pick_column = (node_column[:, None] == eight).astype(jnp.float32)
    pick_row = (node_row[:, None] == eight).astype(jnp.float32)
    same_element = element[:, None] == element[None, :]
    along_xi = jnp.dot(
        jnp.dot(pick_column, chebyshev.T, precision=highest_precision),
        pick_column.T,
        precision=highest_precision,
    )
    along_eta = jnp.dot(
        jnp.dot(pick_row, chebyshev.T, precision=highest_precision),
        pick_row.T,
        precision=highest_precision,
    )
    xi_table = jnp.where(same_element & (node_row[:, None] == node_row[None, :]), along_xi, 0.0)
    eta_table = jnp.where(
        same_element & (node_column[:, None] == node_column[None, :]), along_eta, 0.0
    )
    return (xi_table, eta_table)


def plane_slopes(values, xi_table, eta_table, main_part, cross_part):
    flat_values = values.reshape(-1, 128)
    xi_slope = jnp.dot(flat_values, xi_table, precision=highest_precision).reshape(values.shape)
    eta_slope = jnp.dot(flat_values, eta_table, precision=highest_precision).reshape(values.shape)
    grad_x = main_part[0] * xi_slope + cross_part[0] * eta_slope
    grad_y = cross_part[1] * xi_slope + main_part[1] * eta_slope
    return (grad_x, grad_y)


def general_device(velocity, metric_main, metric_cross, stiffness, mass, precond, trace_map):
    rows_dev = velocity.shape[1]
    points = velocity.shape[2]
    patch_dev = trace_map.shape[0]
    width = stiffness.shape[1]
    trace_width = trace_map.shape[2]
    modes_dev = rows_dev // 2
    chebyshev = jnp.asarray(chebyshev_matrix(), jnp.float32)
    xi_table, eta_table = general_plane(chebyshev)
    basis_table, slope_table, forward, wave_all = general_spanwise()
    wave_rows = lax.dynamic_slice_in_dim(wave_all, lax.axis_index("mode") * rows_dev, rows_dev)
    damping = (1.0 + viscous_step * wave_rows * wave_rows)[None, :, None, None]
    patches = stiffness.reshape(patch_dev, width, width)
    inverse = precond.reshape(modes_dev, patch_dev, width, width)
    patch_mass = mass.reshape(patch_dev, width)
    point_numbers = jnp.arange(width, dtype=jnp.int32)[None, None, :]
    left_pick = (trace_map[:, 0][:, :, None] == point_numbers).astype(jnp.float32)
    right_pick = (trace_map[:, 1][:, :, None] == point_numbers).astype(jnp.float32)
    global_patch = lax.axis_index("elem") * patch_dev + jnp.arange(patch_dev)
    last_patch = patch_dev * lax.axis_size("elem") - 1
    left_gain = (global_patch > 0).astype(jnp.float32)[:, None]
    right_gain = (global_patch < last_patch).astype(jnp.float32)[:, None]
    multiplicity = (
        1.0 + left_gain * jnp.sum(left_pick, axis=1) + right_gain * jnp.sum(right_pick, axis=1)
    )
    weight = relaxation / (multiplicity * multiplicity)
    share = points // lax.axis_size("mode")
    main_share = lax.dynamic_slice_in_dim(metric_main, lax.axis_index("mode") * share, share, 1)
    cross_share = lax.dynamic_slice_in_dim(metric_cross, lax.axis_index("mode") * share, share, 1)

    def assemble(values):
        left_values = jnp.einsum("crpl,pjl->crpj", values, left_pick, precision=highest_precision)
        right_values = jnp.einsum("crpl,pjl->crpj", values, right_pick, precision=highest_precision)
        upward = shifted(right_values[:, :, -1].reshape(-1), "elem", 1)
        downward = shifted(left_values[:, :, 0].reshape(-1), "elem", -1)
        from_below = jnp.concatenate(
            [upward.reshape(3, rows_dev, 1, trace_width), right_values[:, :, :-1]], axis=2
        )
        from_above = jnp.concatenate(
            [left_values[:, :, 1:], downward.reshape(3, rows_dev, 1, trace_width)], axis=2
        )
        below_points = jnp.einsum(
            "crpj,pjl->crpl", from_below, left_pick, precision=highest_precision
        )
        above_points = jnp.einsum(
            "crpj,pjl->crpl", from_above, right_pick, precision=highest_precision
        )
        return values + below_points + above_points

    state = velocity
    for time_level in range(STEPS):
        coefficients = lax.all_to_all(state, "mode", split_axis=2, concat_axis=1, tiled=True)
        grad_x, grad_y = plane_slopes(coefficients, xi_table, eta_table, main_share, cross_share)
        plane_part = jnp.einsum(
            "frp,zr->fpz",
            jnp.concatenate([coefficients, grad_x, grad_y], axis=0),
            basis_table,
            precision=highest_precision,
        )
        spanwise_part = jnp.einsum(
            "frp,zr->fpz", coefficients, slope_table, precision=highest_precision
        )
        physical = jnp.concatenate([plane_part, spanwise_part], axis=0)
        advection = (
            physical[0:1] * physical[3:6]
            + physical[1:2] * physical[6:9]
            + physical[2:3] * physical[9:12]
        )
        advection_points = jnp.einsum(
            "ipz,rz->irp", advection, forward, precision=highest_precision
        )
        advection_hat = lax.all_to_all(
            advection_points, "mode", split_axis=1, concat_axis=2, tiled=True
        )
        source = (state - time_step * advection_hat).reshape(3, rows_dev, patch_dev, width)
        local_term = patch_mass * source
        iterate = jnp.zeros_like(source)
        for sweep_number in range(ITERS):
            if sweep_number == 0:
                residual = assemble(local_term)
            else:
                stiff_part = jnp.einsum(
                    "pij,crpj->crpi", patches, iterate, precision=highest_precision
                )
                residual = assemble(
                    local_term - viscous_step * stiff_part - damping * patch_mass * iterate
                )
            grouped = residual.reshape(3, modes_dev, 2, patch_dev, width)
            correction = jnp.einsum(
                "kpij,ckhpj->ckhpi", inverse, grouped, precision=highest_precision
            ).reshape(3, rows_dev, patch_dev, width)
            iterate = iterate + weight * assemble(correction)
        state = iterate.reshape(3, rows_dev, points)
    return state


def solution(mesh):
    return jax.shard_map(
        on_device,
        mesh=mesh,
        in_specs=(
            P(None, "mode", "elem"),
            P(None, "elem"),
            P(None, "elem"),
            P("elem", None),
            P("elem"),
            P("mode", "elem", None),
            P("elem", None, None),
        ),
        out_specs=P(None, "mode", "elem"),
        check_vma=False,
    )
```

```python
import functools
import math

import jax
import jax.numpy as jnp
import numpy as np
from jax import lax
from jax.experimental import pallas as pl
from jax.experimental.pallas import tpu as pltpu
from jax.sharding import PartitionSpec as P

NZ = 256
STEPS = 4
ITERS = 4
LANES = 128

viscous_step = 0.5
time_step = 0.02
relaxation = 0.8
f32 = jnp.float32
bf16 = jnp.bfloat16
MODES = 64
KZ = 128
highest_precision = lax.Precision.HIGHEST


def chebyshev_matrix():
    node_points = np.cos(np.pi * np.arange(8) / 7.0)
    weights = np.where((np.arange(8) == 0) | (np.arange(8) == 7), 2.0, 1.0)
    parity = np.where((np.arange(8)[:, None] + np.arange(8)[None, :]) % 2 == 0, 1.0, -1.0)
    identity = np.eye(8)
    spacing = node_points[:, None] - node_points[None, :] + identity
    off_diagonal = weights[:, None] / weights[None, :] * parity / spacing * (1.0 - identity)
    return off_diagonal - identity * off_diagonal.sum(axis=1)[:, None]


def pair(table):
    table = np.asarray(table, np.float32)
    high = table.astype(bf16)
    low = (table - high.astype(np.float32)).astype(bf16)
    return high, low


def spanwise_tables(modes):
    angle = 2.0 * math.pi / NZ * (np.arange(NZ)[:, None] * np.arange(modes)[None, :] % NZ)
    rate = 4.0 * np.arange(modes) / modes
    cosine, sine = np.cos(angle), np.sin(angle)
    basis = np.concatenate([cosine, sine], axis=1)
    slope = np.concatenate([-rate * sine, rate * cosine], axis=1)
    factor = np.full(2 * modes, 2.0 / NZ)
    factor[0] = 1.0 / NZ
    forward = basis.T * factor[:, None]

    def left_three(table):
        high, low = pair(table)
        return np.concatenate([high, low, high], axis=1)

    return left_three(basis), left_three(slope), np.stack(pair(forward))


def plane_tables():
    chebyshev = chebyshev_matrix()
    position = np.arange(LANES)
    column, row, element = position % 8, position // 8 % 8, position // 64
    same = element[:, None] == element[None, :]
    xi = np.where(same & (row[:, None] == row[None, :]), chebyshev.T[column][:, column], 0.0)
    eta = np.where(same & (column[:, None] == column[None, :]), chebyshev.T[row][:, row], 0.0)
    return np.stack(pair(np.concatenate([xi, eta], axis=1)))


def row_order(modes):
    move = np.zeros((modes * 8, 6 * modes), np.float32)
    for field in range(6):
        for mode in range(modes):
            move[mode * 8 + field, field * modes + mode] = 1.0
    shuffle = np.zeros((6 * modes, 6 * modes), np.float32)
    for c in range(3):
        for half in range(2):
            for mode in range(modes):
                shuffle[(2 * c + half) * modes + mode, (c * modes + mode) * 2 + half] = 1.0
    return [table.astype(bf16) for table in (move, move.T, shuffle, shuffle.T @ move.T)]


def dot(a, b):
    return lax.dot_general(a, b, (((1,), (0,)), ((), ())), preferred_element_type=f32)


def split(value):
    high = value.astype(bf16)
    return high, (value - high.astype(f32)).astype(bf16)


def both(value):
    high = value.astype(bf16).astype(f32)
    low = value - high
    tiles = []
    for start in range(0, value.shape[0], 8):
        tiles += [high[start : start + 8], low[start : start + 8]]
    return jnp.concatenate(tiles, axis=0).astype(bf16)


def folded(value):
    tiles = [
        value[start : start + 8] + value[start + 8 : start + 16]
        for start in range(0, value.shape[0], 16)
    ]
    return jnp.concatenate(tiles, axis=0)


def product(value, high, low):
    parts = both(value)
    return folded(dot(parts, high) + dot(parts, low))


def moved(value, one_hot):
    return folded(dot(both(value), one_hot))


def reordered(move, value):
    high, low = split(value)
    return dot(move, high) + dot(move, low)


def exactly(move, value):
    high, low = split(value)
    rest = (value - high.astype(f32) - low.astype(f32)).astype(bf16)
    return dot(move, high) + (dot(move, low) + dot(move, rest))


def kernel(
    ranks,
    depth,
    modes,
    patches,
    width,
    trace,
    share,
    velocity,
    metric_main,
    metric_cross,
    stiffness,
    mass,
    slots,
    tables,
    forward,
    plane,
    move,
    back,
    enter,
    leave,
    precond,
    out,
    raw,
    inverse_high,
    inverse_low,
    stiff_high,
    stiff_low,
    across,
    edge_high,
    edge_low,
    rows_high,
    rows_low,
    gate_high,
    gate_low,
    pick,
    pick_back,
    corner_out,
    corner_in,
    corner_high,
    corner_low,
    state,
    coef,
    hat,
    returned,
    local,
    damped,
    weight,
    iterate,
    note_out,
    note_in,
    raw_sem,
    own_sem,
    coef_send,
    hat_send,
    coef_sem,
    hat_sem,
    note_send,
    note_recv,
    corner_send,
    corner_recv,
):
    me = lax.axis_index("mode")
    place = lax.axis_index("elem")
    has = (place > 0, place < depth - 1)
    beside = (place - 1, place + 1)
    rows = 8 * modes
    wide = modes * trace

    def patch_of(p):
        return pl.ds(p * width, width)

    for k in range(modes):
        for p in range(patches):
            pltpu.make_async_copy(
                precond.at[k, patch_of(p), :], raw.at[k, patch_of(p), :], raw_sem.at[k, p]
            ).start()

    note_in[...] = jnp.zeros_like(note_in)
    corner_in[...] = jnp.zeros_like(corner_in)
    state[...] = exactly(enter[...], velocity[...].reshape(6 * modes, patches * width)).reshape(
        6, modes, patches * width
    )

    barrier = pltpu.get_barrier_semaphore()
    for offset in range(1, ranks):
        pl.semaphore_signal(
            barrier, 1, device_id={"mode": lax.rem(me + offset, ranks)},
            device_id_type=pl.DeviceIdType.MESH,
        )
    for side in range(2):
        @pl.when(has[side])
        def _():
            pl.semaphore_signal(
                barrier, 1, device_id={"elem": beside[side]}, device_id_type=pl.DeviceIdType.MESH
            )
    near_side = (jnp.minimum(place, 1), jnp.minimum(depth - 1 - place, 1))
    near_count = [side.astype(f32) for side in near_side]
    pl.semaphore_wait(barrier, ranks - 1 + near_side[0] + near_side[1])

    def points_of(rank):
        return pl.ds(pl.multiple_of(rank * share, share), share)

    def modes_of(rank):
        return pl.ds(pl.multiple_of(rank * modes, modes), modes)

    def coef_copy(offset):
        to = lax.rem(me + offset, ranks)
        return pltpu.make_async_remote_copy(
            src_ref=state.at[:, :, points_of(to)],
            dst_ref=coef.at[:, modes_of(me), :],
            send_sem=coef_send.at[offset],
            recv_sem=coef_sem.at[offset],
            device_id={"mode": to},
            device_id_type=pl.DeviceIdType.MESH,
        )

    def hat_copy(offset, c):
        to = lax.rem(me + offset, ranks)
        return pltpu.make_async_remote_copy(
            src_ref=hat.at[pl.ds(2 * c, 2), modes_of(to), :],
            dst_ref=returned.at[pl.ds(2 * c, 2), :, points_of(me)],
            send_sem=hat_send.at[c, offset],
            recv_sem=hat_sem.at[c, offset],
            device_id={"mode": to},
            device_id_type=pl.DeviceIdType.MESH,
        )

    def own_coef():
        return pltpu.make_async_copy(
            state.at[:, :, points_of(me)], coef.at[:, modes_of(me), :], own_sem.at[0]
        )

    def own_hat():
        return pltpu.make_async_copy(
            hat.at[:, modes_of(me), :], returned.at[:, :, points_of(me)], own_sem.at[1]
        )

    def send_coef():
        for offset in range(1, ranks):
            coef_copy(offset).start()
        own_coef().start()

    def note_copy(side, slot):
        return pltpu.make_async_remote_copy(
            src_ref=note_out.at[side],
            dst_ref=note_in.at[slot, 1 - side],
            send_sem=note_send.at[side],
            recv_sem=note_recv.at[slot, 1 - side],
            device_id={"elem": beside[side]},
            device_id_type=pl.DeviceIdType.MESH,
        )

    def corner_copy(side):
        return pltpu.make_async_remote_copy(
            src_ref=corner_out.at[side],
            dst_ref=corner_in.at[1 - side],
            send_sem=corner_send.at[side],
            recv_sem=corner_recv.at[1 - side],
            device_id={"elem": beside[side]},
            device_id_type=pl.DeviceIdType.MESH,
        )

    def note_wait(side, slot):
        note_copy(side, slot).wait_send()
        pltpu.make_async_remote_copy(
            src_ref=note_out.at[side],
            dst_ref=note_in.at[slot, side],
            send_sem=note_send.at[side],
            recv_sem=note_recv.at[slot, side],
            device_id={"elem": beside[side]},
            device_id_type=pl.DeviceIdType.MESH,
        ).wait_recv()

    def corner_wait(side):
        corner_copy(side).wait_send()
        pltpu.make_async_remote_copy(
            src_ref=corner_out.at[side],
            dst_ref=corner_in.at[side],
            send_sem=corner_send.at[side],
            recv_sem=corner_recv.at[side],
            device_id={"elem": beside[side]},
            device_id_type=pl.DeviceIdType.MESH,
        ).wait_recv()

    send_coef()

    edge_patch = (0, patches - 1)
    point = lax.broadcasted_iota(jnp.int32, (width, LANES), 0)
    for p in range(patches):
        stiff_high[p], stiff_low[p] = split(viscous_step * stiffness[patch_of(p), :])
        multiplicity = jnp.ones((1, width), f32)
        for side in range(2):
            for kind in range(2):
                line = (p * 2 + side) * 2 + kind
                one_hot = jnp.where(slots[line : line + 1, :] == point, 1.0, 0.0)
                turned = one_hot.T
                pick[p, side, kind] = one_hot.astype(bf16)
                pick_back[p, side, kind] = turned.astype(bf16)
                if kind == 0:
                    gain = near_count[side] if p == edge_patch[side] else 1.0
                    multiplicity += gain * jnp.sum(turned, axis=0, keepdims=True)
        weight[:, patch_of(p)] = relaxation / (multiplicity * multiplicity)
    for p in range(patches - 1):
        across[p, 0] = dot(pick[p, 1, 0], pick_back[p + 1, 0, 0]).astype(bf16)
        across[p, 1] = dot(pick[p + 1, 0, 0], pick_back[p, 1, 0]).astype(bf16)
    number = lax.broadcasted_iota(jnp.int32, (rows, 1), 0) // 8 + me * modes
    rate = 4.0 * number.astype(f32) / (modes * ranks)
    damped[...] = (1.0 + viscous_step * rate * rate) * mass[...]

    def prepare(k, carry):
        span = pl.ds(pl.multiple_of(k * trace, trace), trace)
        for p in range(patches):
            pltpu.make_async_copy(
                precond.at[k, patch_of(p), :], raw.at[k, patch_of(p), :], raw_sem.at[k, p]
            ).wait()
            block = raw[k, patch_of(p), :]
            high, low = split(block.T)
            inverse_high[k, p] = high
            inverse_low[k, p] = low
            plain_high, plain_low = split(block)
            for side in range(2):
                if p == edge_patch[side]:
                    choose = pick_back[p, side, 0, :trace, :]
                    edge_high[side, span, :] = dot(choose, high).astype(bf16)
                    edge_low[side, span, :] = dot(choose, low).astype(bf16)
                    rows_high[side, span, :] = dot(choose, plain_high)
                    rows_low[side, span, :] = dot(choose, plain_low)
        return carry

    lax.fori_loop(0, modes, prepare, 0)
    for side in range(2):
        choose = pick[edge_patch[side], side, 1]
        corner_out[side] = dot(edge_high[side], choose) + dot(edge_low[side], choose)

        @pl.when(has[side])
        def _():
            corner_copy(side).start()
    for side in range(2):
        gate_high[side, :, :wide] = rows_high[side].T.astype(bf16)
        gate_high[side, :, wide:] = pick[edge_patch[side], side, 0]
        gate_low[side] = rows_low[side].T.astype(bf16)
    for side in range(2):
        @pl.when(has[side])
        def _():
            corner_wait(side)
        corner_high[side], corner_low[side] = split(corner_in[side])

    lane = lax.broadcasted_iota(jnp.int32, (rows, LANES), 1)
    block_mask = (
        lax.broadcasted_iota(jnp.int32, (rows, wide), 0) // 8
        == lax.broadcasted_iota(jnp.int32, (rows, wide), 1) // trace
    )

    def repeated(value):
        total = value
        for turn in range(1, LANES // trace):
            total = total + pltpu.roll(value, turn * trace, 1)
        return total

    def spread(note):
        total = repeated(jnp.where(lane < trace, note, 0.0))
        tiled = jnp.concatenate([total] * (wide // LANES), axis=1)
        return jnp.where(block_mask, tiled, 0.0)

    def noted(parts, side):
        sent = folded(dot(parts, gate_high[side]))
        traced = sent[:, :wide] + folded(dot(parts, gate_low[side]))
        traced = jnp.where(block_mask, traced, 0.0)
        total = traced[:, :LANES]
        for start in range(LANES, wide, LANES):
            total = total + traced[:, start : start + LANES]
        return sent[:, wide:] + jnp.where(lane >= trace, repeated(total), 0.0)

    def advect():
        for offset in range(1, ranks):
            coef_copy(offset).wait_recv()
        own_coef().wait()
        each = 2 * modes * ranks
        fields = coef[...].reshape(3 * each, share)
        high, low = split(fields)
        slopes = dot(high, plane[0]) + dot(low, plane[0]) + dot(high, plane[1])
        xi, eta = slopes[:, :share], slopes[:, share:]
        mine = points_of(me)
        grad_x = metric_main[0:1, mine] * xi + metric_cross[0:1, mine] * eta
        grad_y = metric_cross[1:2, mine] * xi + metric_main[1:2, mine] * eta

        def physical(table, values):
            high, low = split(jnp.concatenate(values, axis=1))
            return dot(table, jnp.concatenate([high, high, low], axis=0))

        def part(value, c):
            return value[c * each : (c + 1) * each]

        plain = physical(tables[...], [part(fields, c) for c in range(3)])
        u, v, w = (plain[:NZ, c * share : (c + 1) * share] for c in range(3))
        for c in range(3):
            slope = physical(tables[:NZ], [part(grad_x, c), part(grad_y, c)])
            advection = (
                u * slope[:, :share]
                + v * slope[:, share:]
                + w * plain[NZ:, c * share : (c + 1) * share]
            )
            high, low = split(advection)
            total = dot(forward[0], high) + dot(forward[0], low) + dot(forward[1], high)
            hat[pl.ds(2 * c, 2)] = total.reshape(2, modes * ranks, share)
            for offset in range(1, ranks):
                hat_copy(offset, c).start()
        own_hat().start()
        for offset in range(1, ranks):
            coef_copy(offset).wait_send()
            for c in range(3):
                hat_copy(offset, c).wait_recv()
        own_hat().wait()
        for offset in range(1, ranks):
            for c in range(3):
                hat_copy(offset, c).wait_send()
        source = (state[...] - time_step * returned[...]).reshape(6 * modes, patches * width)
        local[...] = mass[...] * reordered(move[...], source)

    def assembled(parts):
        result = list(parts)
        for p in range(patches - 1):
            result[p + 1] = result[p + 1] + moved(parts[p], across[p, 0])
            result[p] = result[p] + moved(parts[p + 1], across[p, 1])
        return result

    def sweep(number, first):
        slot = lax.rem(number, 2)
        terms = []
        for p in range(patches):
            term = local[:, patch_of(p)]
            if not first:
                value = iterate[:, patch_of(p)]
                term = (
                    term
                    - product(value, stiff_high[p], stiff_low[p])
                    - damped[:, patch_of(p)] * value
                )
            terms.append(term)
        lines = [both(term) for term in assembled(terms)]
        notes = []
        for side in range(2):
            note = noted(lines[edge_patch[side]], side)
            note_out[side] = note
            notes.append(note)
        for side in range(2):
            @pl.when(has[side])
            def _():
                note_copy(side, slot).start()
        parts = []
        for p in range(patches):
            found = []
            for k in range(modes):
                line = lines[p][k * 16 : (k + 1) * 16]
                found.append(dot(line, inverse_high[k, p]) + dot(line, inverse_low[k, p]))
            parts.append(folded(jnp.concatenate(found, axis=0)))
        near = [product(spread(notes[side]), corner_high[side], corner_low[side]) for side in range(2)]
        for side in range(2):
            @pl.when(has[side])
            def _():
                note_wait(side, slot)
        gains = []
        for side in range(2):
            p = edge_patch[side]
            note = note_in[slot, side]
            parts[p] = parts[p] + product(spread(note), edge_high[side], edge_low[side])
            gains.append(moved(note + near[side], pick_back[p, side, 1]))
        total = assembled(parts)
        for side in range(2):
            p = edge_patch[side]
            total[p] = total[p] + gains[side]
        for p in range(patches):
            step = weight[:, patch_of(p)] * total[p]
            iterate[:, patch_of(p)] = step if first else iterate[:, patch_of(p)] + step

    def later_sweep(number, carry):
        sweep(number, False)
        return carry

    def level(number, carry):
        advect()
        sweep(0, True)
        lax.fori_loop(1, ITERS, later_sweep, 0)
        state[...] = reordered(back[...], iterate[...]).reshape(6, modes, patches * width)

        @pl.when(number < STEPS - 1)
        def _():
            send_coef()

        return carry

    lax.fori_loop(0, STEPS, level, 0)
    out[...] = exactly(leave[...], iterate[...]).reshape(3, 2 * modes, patches * width)


def on_device(velocity, metric_main, metric_cross, stiffness, mass, precond, trace_map):
    ranks, depth = lax.axis_size("mode"), lax.axis_size("elem")
    rows, points = velocity.shape[1:]
    modes = rows // 2
    patches, _, trace = trace_map.shape
    width = stiffness.shape[1]
    share = points // ranks
    if modes % 8 or share != LANES or LANES % trace or (modes * trace) % LANES or patches < 2:
        return general_device(
            velocity, metric_main, metric_cross, stiffness, mass, precond, trace_map
        )
    slots = jnp.stack(
        [
            jnp.pad(trace_map, ((0, 0), (0, 0), (0, LANES - trace)), constant_values=-1),
            jnp.pad(trace_map, ((0, 0), (0, 0), (trace, LANES - 2 * trace)), constant_values=-1),
        ],
        axis=2,
    )
    basis, slope, forward = spanwise_tables(modes * ranks)
    vmem = pl.BlockSpec(memory_space=pltpu.VMEM)
    wide = modes * trace
    blocks = (modes, patches, width, width)
    return pl.pallas_call(
        functools.partial(kernel, ranks, depth, modes, patches, width, trace, share),
        out_shape=jax.ShapeDtypeStruct(velocity.shape, f32),
        in_specs=[vmem] * 13 + [pl.BlockSpec(memory_space=pl.ANY)],
        out_specs=vmem,
        scratch_shapes=[
            pltpu.VMEM((modes, patches * width, width), f32),
            pltpu.VMEM(blocks, bf16),
            pltpu.VMEM(blocks, bf16),
            pltpu.VMEM((patches, width, width), bf16),
            pltpu.VMEM((patches, width, width), bf16),
            pltpu.VMEM((patches - 1, 2, width, width), bf16),
            pltpu.VMEM((2, wide, width), bf16),
            pltpu.VMEM((2, wide, width), bf16),
            pltpu.VMEM((2, wide, width), f32),
            pltpu.VMEM((2, wide, width), f32),
            pltpu.VMEM((2, width, wide + LANES), bf16),
            pltpu.VMEM((2, width, wide), bf16),
            pltpu.VMEM((patches, 2, 2, width, LANES), bf16),
            pltpu.VMEM((patches, 2, 2, LANES, width), bf16),
            pltpu.VMEM((2, wide, LANES), f32),
            pltpu.VMEM((2, wide, LANES), f32),
            pltpu.VMEM((2, wide, LANES), bf16),
            pltpu.VMEM((2, wide, LANES), bf16),
            pltpu.VMEM((6, modes, points), f32),
            pltpu.VMEM((6, modes * ranks, share), f32),
            pltpu.VMEM((6, modes * ranks, share), f32),
            pltpu.VMEM((6, modes, points), f32),
            pltpu.VMEM((8 * modes, points), f32),
            pltpu.VMEM((8 * modes, points), f32),
            pltpu.VMEM((1, points), f32),
            pltpu.VMEM((8 * modes, points), f32),
            pltpu.VMEM((2, 8 * modes, LANES), f32),
            pltpu.VMEM((2, 2, 8 * modes, LANES), f32),
            pltpu.SemaphoreType.DMA((modes, patches)),
            pltpu.SemaphoreType.DMA((2,)),
            pltpu.SemaphoreType.DMA((ranks,)),
            pltpu.SemaphoreType.DMA((3, ranks)),
            pltpu.SemaphoreType.DMA((ranks,)),
            pltpu.SemaphoreType.DMA((3, ranks)),
            pltpu.SemaphoreType.DMA((2,)),
            pltpu.SemaphoreType.DMA((2, 2)),
            pltpu.SemaphoreType.DMA((2,)),
            pltpu.SemaphoreType.DMA((2,)),
        ],
        compiler_params=pltpu.CompilerParams(
            collective_id=0, has_side_effects=True, vmem_limit_bytes=56 * 1024 * 1024
        ),
    )(
        velocity,
        metric_main,
        metric_cross,
        stiffness,
        mass.reshape(1, points),
        slots.reshape(patches * 4, LANES),
        jnp.asarray(np.concatenate([basis, slope], axis=0)),
        jnp.asarray(forward),
        jnp.asarray(plane_tables()),
        *[jnp.asarray(table) for table in row_order(modes)],
        precond,
    )


def shifted(value, axis, steps):
    count = lax.axis_size(axis)
    initial, last = (max(0, -steps), min(count, count - steps))
    return lax.ppermute(value, axis, [(source, source + steps) for source in range(initial, last)])


def general_spanwise():
    spanwise = jnp.arange(NZ, dtype=jnp.int32)
    row_numbers = jnp.arange(KZ, dtype=jnp.int32)
    wavenumber = row_numbers // 2
    product = spanwise[:, None] * wavenumber[None, :] % NZ
    phase_angle = 2.0 * math.pi / NZ * product.astype(jnp.float32)
    is_sine = (row_numbers % 2 == 1)[None, :]
    basis_table = jnp.where(is_sine, jnp.sin(phase_angle), jnp.cos(phase_angle))
    wave_rate = 4.0 * wavenumber.astype(jnp.float32) / MODES
    slope_table = jnp.where(
        is_sine,
        wave_rate[None, :] * jnp.cos(phase_angle),
        -wave_rate[None, :] * jnp.sin(phase_angle),
    )
    norm_factor = jnp.where(row_numbers == 0, 1.0 / NZ, 2.0 / NZ).astype(jnp.float32)
    forward = basis_table.T * norm_factor[:, None]
    return (basis_table, slope_table, forward, wave_rate)


def general_plane(chebyshev):
    position = jnp.arange(128, dtype=jnp.int32)
    node_column = position % 8
    node_row = position // 8 % 8
    element = position // 64
    eight = jnp.arange(8, dtype=jnp.int32)[None, :]
    pick_column = (node_column[:, None] == eight).astype(jnp.float32)
    pick_row = (node_row[:, None] == eight).astype(jnp.float32)
    same_element = element[:, None] == element[None, :]
    along_xi = jnp.dot(
        jnp.dot(pick_column, chebyshev.T, precision=highest_precision),
        pick_column.T,
        precision=highest_precision,
    )
    along_eta = jnp.dot(
        jnp.dot(pick_row, chebyshev.T, precision=highest_precision),
        pick_row.T,
        precision=highest_precision,
    )
    xi_table = jnp.where(same_element & (node_row[:, None] == node_row[None, :]), along_xi, 0.0)
    eta_table = jnp.where(
        same_element & (node_column[:, None] == node_column[None, :]), along_eta, 0.0
    )
    return (xi_table, eta_table)


def plane_slopes(values, xi_table, eta_table, main_part, cross_part):
    flat_values = values.reshape(-1, 128)
    xi_slope = jnp.dot(flat_values, xi_table, precision=highest_precision).reshape(values.shape)
    eta_slope = jnp.dot(flat_values, eta_table, precision=highest_precision).reshape(values.shape)
    grad_x = main_part[0] * xi_slope + cross_part[0] * eta_slope
    grad_y = cross_part[1] * xi_slope + main_part[1] * eta_slope
    return (grad_x, grad_y)


def general_device(velocity, metric_main, metric_cross, stiffness, mass, precond, trace_map):
    rows_dev = velocity.shape[1]
    points = velocity.shape[2]
    patch_dev = trace_map.shape[0]
    width = stiffness.shape[1]
    trace_width = trace_map.shape[2]
    modes_dev = rows_dev // 2
    chebyshev = jnp.asarray(chebyshev_matrix(), jnp.float32)
    xi_table, eta_table = general_plane(chebyshev)
    basis_table, slope_table, forward, wave_all = general_spanwise()
    wave_rows = lax.dynamic_slice_in_dim(wave_all, lax.axis_index("mode") * rows_dev, rows_dev)
    damping = (1.0 + viscous_step * wave_rows * wave_rows)[None, :, None, None]
    patches = stiffness.reshape(patch_dev, width, width)
    inverse = precond.reshape(modes_dev, patch_dev, width, width)
    patch_mass = mass.reshape(patch_dev, width)
    point_numbers = jnp.arange(width, dtype=jnp.int32)[None, None, :]
    left_pick = (trace_map[:, 0][:, :, None] == point_numbers).astype(jnp.float32)
    right_pick = (trace_map[:, 1][:, :, None] == point_numbers).astype(jnp.float32)
    global_patch = lax.axis_index("elem") * patch_dev + jnp.arange(patch_dev)
    last_patch = patch_dev * lax.axis_size("elem") - 1
    left_gain = (global_patch > 0).astype(jnp.float32)[:, None]
    right_gain = (global_patch < last_patch).astype(jnp.float32)[:, None]
    multiplicity = (
        1.0 + left_gain * jnp.sum(left_pick, axis=1) + right_gain * jnp.sum(right_pick, axis=1)
    )
    weight = relaxation / (multiplicity * multiplicity)
    share = points // lax.axis_size("mode")
    main_share = lax.dynamic_slice_in_dim(metric_main, lax.axis_index("mode") * share, share, 1)
    cross_share = lax.dynamic_slice_in_dim(metric_cross, lax.axis_index("mode") * share, share, 1)

    def assemble(values):
        left_values = jnp.einsum("crpl,pjl->crpj", values, left_pick, precision=highest_precision)
        right_values = jnp.einsum("crpl,pjl->crpj", values, right_pick, precision=highest_precision)
        upward = shifted(right_values[:, :, -1].reshape(-1), "elem", 1)
        downward = shifted(left_values[:, :, 0].reshape(-1), "elem", -1)
        from_below = jnp.concatenate(
            [upward.reshape(3, rows_dev, 1, trace_width), right_values[:, :, :-1]], axis=2
        )
        from_above = jnp.concatenate(
            [left_values[:, :, 1:], downward.reshape(3, rows_dev, 1, trace_width)], axis=2
        )
        below_points = jnp.einsum(
            "crpj,pjl->crpl", from_below, left_pick, precision=highest_precision
        )
        above_points = jnp.einsum(
            "crpj,pjl->crpl", from_above, right_pick, precision=highest_precision
        )
        return values + below_points + above_points

    state = velocity
    for time_level in range(STEPS):
        coefficients = lax.all_to_all(state, "mode", split_axis=2, concat_axis=1, tiled=True)
        grad_x, grad_y = plane_slopes(coefficients, xi_table, eta_table, main_share, cross_share)
        plane_part = jnp.einsum(
            "frp,zr->fpz",
            jnp.concatenate([coefficients, grad_x, grad_y], axis=0),
            basis_table,
            precision=highest_precision,
        )
        spanwise_part = jnp.einsum(
            "frp,zr->fpz", coefficients, slope_table, precision=highest_precision
        )
        physical = jnp.concatenate([plane_part, spanwise_part], axis=0)
        advection = (
            physical[0:1] * physical[3:6]
            + physical[1:2] * physical[6:9]
            + physical[2:3] * physical[9:12]
        )
        advection_points = jnp.einsum(
            "ipz,rz->irp", advection, forward, precision=highest_precision
        )
        advection_hat = lax.all_to_all(
            advection_points, "mode", split_axis=1, concat_axis=2, tiled=True
        )
        source = (state - time_step * advection_hat).reshape(3, rows_dev, patch_dev, width)
        local_term = patch_mass * source
        iterate = jnp.zeros_like(source)
        for sweep_number in range(ITERS):
            if sweep_number == 0:
                residual = assemble(local_term)
            else:
                stiff_part = jnp.einsum(
                    "pij,crpj->crpi", patches, iterate, precision=highest_precision
                )
                residual = assemble(
                    local_term - viscous_step * stiff_part - damping * patch_mass * iterate
                )
            grouped = residual.reshape(3, modes_dev, 2, patch_dev, width)
            correction = jnp.einsum(
                "kpij,ckhpj->ckhpi", inverse, grouped, precision=highest_precision
            ).reshape(3, rows_dev, patch_dev, width)
            iterate = iterate + weight * assemble(correction)
        state = iterate.reshape(3, rows_dev, points)
    return state


def solution(mesh):
    return jax.shard_map(
        on_device,
        mesh=mesh,
        in_specs=(
            P(None, "mode", "elem"),
            P(None, "elem"),
            P(None, "elem"),
            P("elem", None),
            P("elem"),
            P("mode", "elem", None),
            P("elem", None, None),
        ),
        out_specs=P(None, "mode", "elem"),
        check_vma=False,
    )
```

```python
import functools
import math

import jax
import jax.numpy as jnp
import numpy as np
from jax import lax
from jax.experimental import pallas as pl
from jax.experimental.pallas import tpu as pltpu
from jax.sharding import PartitionSpec as P

NZ = 256
STEPS = 4
ITERS = 4
LANES = 128

viscous_step = 0.5
time_step = 0.02
relaxation = 0.8
f32 = jnp.float32
bf16 = jnp.bfloat16
MODES = 64
KZ = 128
highest_precision = lax.Precision.HIGHEST


def chebyshev_matrix():
    node_points = np.cos(np.pi * np.arange(8) / 7.0)
    weights = np.where((np.arange(8) == 0) | (np.arange(8) == 7), 2.0, 1.0)
    parity = np.where((np.arange(8)[:, None] + np.arange(8)[None, :]) % 2 == 0, 1.0, -1.0)
    identity = np.eye(8)
    spacing = node_points[:, None] - node_points[None, :] + identity
    off_diagonal = weights[:, None] / weights[None, :] * parity / spacing * (1.0 - identity)
    return off_diagonal - identity * off_diagonal.sum(axis=1)[:, None]


def pair(table):
    table = np.asarray(table, np.float32)
    high = table.astype(bf16)
    low = (table - high.astype(np.float32)).astype(bf16)
    return high, low


def spanwise_tables(modes):
    angle = 2.0 * math.pi / NZ * (np.arange(NZ)[:, None] * np.arange(modes)[None, :] % NZ)
    rate = 4.0 * np.arange(modes) / modes
    cosine, sine = np.cos(angle), np.sin(angle)
    basis = np.concatenate([cosine, sine], axis=1)
    slope = np.concatenate([-rate * sine, rate * cosine], axis=1)
    factor = np.full(2 * modes, 2.0 / NZ)
    factor[0] = 1.0 / NZ
    forward = basis.T * factor[:, None]

    def left_three(table):
        high, low = pair(table)
        return np.concatenate([high, low, high], axis=1)

    return left_three(basis), left_three(slope), np.stack(pair(forward))


def plane_tables():
    chebyshev = chebyshev_matrix()
    position = np.arange(LANES)
    column, row, element = position % 8, position // 8 % 8, position // 64
    same = element[:, None] == element[None, :]
    xi = np.where(same & (row[:, None] == row[None, :]), chebyshev.T[column][:, column], 0.0)
    eta = np.where(same & (column[:, None] == column[None, :]), chebyshev.T[row][:, row], 0.0)
    return np.stack(pair(np.concatenate([xi, eta], axis=1)))


def row_order(modes):
    move = np.zeros((modes * 8, 6 * modes), np.float32)
    for field in range(6):
        for mode in range(modes):
            move[mode * 8 + field, field * modes + mode] = 1.0
    shuffle = np.zeros((6 * modes, 6 * modes), np.float32)
    for c in range(3):
        for half in range(2):
            for mode in range(modes):
                shuffle[(2 * c + half) * modes + mode, (c * modes + mode) * 2 + half] = 1.0
    return [table.astype(bf16) for table in (move, move.T, shuffle, shuffle.T @ move.T)]


def dot(a, b):
    return lax.dot_general(a, b, (((1,), (0,)), ((), ())), preferred_element_type=f32)


def split(value):
    high = value.astype(bf16)
    return high, (value - high.astype(f32)).astype(bf16)


def both(value):
    high = value.astype(bf16).astype(f32)
    low = value - high
    tiles = []
    for start in range(0, value.shape[0], 8):
        tiles += [high[start : start + 8], low[start : start + 8]]
    return jnp.concatenate(tiles, axis=0).astype(bf16)


def folded(value):
    tiles = [
        value[start : start + 8] + value[start + 8 : start + 16]
        for start in range(0, value.shape[0], 16)
    ]
    return jnp.concatenate(tiles, axis=0)


def product(value, high, low):
    parts = both(value)
    return folded(dot(parts, high) + dot(parts, low))


def moved(value, one_hot):
    return folded(dot(both(value), one_hot))


def reordered(move, value):
    high, low = split(value)
    return dot(move, high) + dot(move, low)


def exactly(move, value):
    high, low = split(value)
    rest = (value - high.astype(f32) - low.astype(f32)).astype(bf16)
    return dot(move, high) + (dot(move, low) + dot(move, rest))


def kernel(
    ranks,
    depth,
    modes,
    patches,
    width,
    trace,
    share,
    velocity,
    metric_main,
    metric_cross,
    stiffness,
    mass,
    trace_map,
    tables,
    forward,
    plane,
    move,
    back,
    enter,
    leave,
    precond,
    out,
    raw,
    inverse_high,
    inverse_low,
    stiff_high,
    stiff_low,
    across,
    edge_high,
    edge_low,
    beyond_high,
    beyond_low,
    rows_high,
    rows_low,
    gate_high,
    gate_low,
    pick,
    pick_back,
    corner_out,
    corner_in,
    corner_high,
    corner_low,
    state,
    coef,
    hat,
    returned,
    local,
    damped,
    weight,
    iterate,
    note_out,
    note_in,
    raw_sem,
    own_sem,
    coef_send,
    hat_send,
    coef_sem,
    hat_sem,
    note_send,
    note_recv,
    corner_send,
    corner_recv,
):
    me = lax.axis_index("mode")
    place = lax.axis_index("elem")
    has = (place > 0, place < depth - 1)
    beside = (place - 1, place + 1)
    rows = 8 * modes
    wide = modes * trace

    def patch_of(p):
        return pl.ds(p * width, width)

    for k in range(modes):
        for p in range(patches):
            pltpu.make_async_copy(
                precond.at[k, patch_of(p), :], raw.at[k, patch_of(p), :], raw_sem.at[k, p]
            ).start()

    note_in[...] = jnp.zeros_like(note_in)
    corner_in[...] = jnp.zeros_like(corner_in)
    state[...] = exactly(enter[...], velocity[...].reshape(6 * modes, patches * width)).reshape(
        6, modes, patches * width
    )

    barrier = pltpu.get_barrier_semaphore()
    for offset in range(1, ranks):
        pl.semaphore_signal(
            barrier, 1, device_id={"mode": lax.rem(me + offset, ranks)},
            device_id_type=pl.DeviceIdType.MESH,
        )
    for side in range(2):
        @pl.when(has[side])
        def _():
            pl.semaphore_signal(
                barrier, 1, device_id={"elem": beside[side]}, device_id_type=pl.DeviceIdType.MESH
            )
    near_side = (jnp.minimum(place, 1), jnp.minimum(depth - 1 - place, 1))
    near_count = [side.astype(f32) for side in near_side]
    pl.semaphore_wait(barrier, ranks - 1 + near_side[0] + near_side[1])

    def points_of(rank):
        return pl.ds(pl.multiple_of(rank * share, share), share)

    def modes_of(rank):
        return pl.ds(pl.multiple_of(rank * modes, modes), modes)

    def coef_copy(offset):
        to = lax.rem(me + offset, ranks)
        return pltpu.make_async_remote_copy(
            src_ref=state.at[:, :, points_of(to)],
            dst_ref=coef.at[:, modes_of(me), :],
            send_sem=coef_send.at[offset],
            recv_sem=coef_sem.at[offset],
            device_id={"mode": to},
            device_id_type=pl.DeviceIdType.MESH,
        )

    def hat_copy(offset, c):
        to = lax.rem(me + offset, ranks)
        return pltpu.make_async_remote_copy(
            src_ref=hat.at[pl.ds(2 * c, 2), modes_of(to), :],
            dst_ref=returned.at[pl.ds(2 * c, 2), :, points_of(me)],
            send_sem=hat_send.at[c, offset],
            recv_sem=hat_sem.at[c, offset],
            device_id={"mode": to},
            device_id_type=pl.DeviceIdType.MESH,
        )

    def own_coef():
        return pltpu.make_async_copy(
            state.at[:, :, points_of(me)], coef.at[:, modes_of(me), :], own_sem.at[0]
        )

    def own_hat():
        return pltpu.make_async_copy(
            hat.at[:, modes_of(me), :], returned.at[:, :, points_of(me)], own_sem.at[1]
        )

    def send_coef():
        for offset in range(1, ranks):
            coef_copy(offset).start()
        own_coef().start()

    def note_copy(side, slot):
        return pltpu.make_async_remote_copy(
            src_ref=note_out.at[side],
            dst_ref=note_in.at[slot, 1 - side],
            send_sem=note_send.at[side],
            recv_sem=note_recv.at[slot, 1 - side],
            device_id={"elem": beside[side]},
            device_id_type=pl.DeviceIdType.MESH,
        )

    def corner_copy(side):
        return pltpu.make_async_remote_copy(
            src_ref=corner_out.at[side],
            dst_ref=corner_in.at[1 - side],
            send_sem=corner_send.at[side],
            recv_sem=corner_recv.at[1 - side],
            device_id={"elem": beside[side]},
            device_id_type=pl.DeviceIdType.MESH,
        )

    def note_wait(side, slot):
        note_copy(side, slot).wait_send()
        pltpu.make_async_remote_copy(
            src_ref=note_out.at[side],
            dst_ref=note_in.at[slot, side],
            send_sem=note_send.at[side],
            recv_sem=note_recv.at[slot, side],
            device_id={"elem": beside[side]},
            device_id_type=pl.DeviceIdType.MESH,
        ).wait_recv()

    def corner_wait(side):
        corner_copy(side).wait_send()
        pltpu.make_async_remote_copy(
            src_ref=corner_out.at[side],
            dst_ref=corner_in.at[side],
            send_sem=corner_send.at[side],
            recv_sem=corner_recv.at[side],
            device_id={"elem": beside[side]},
            device_id_type=pl.DeviceIdType.MESH,
        ).wait_recv()

    send_coef()

    edge_patch = (0, patches - 1)
    point = lax.broadcasted_iota(jnp.int32, (width, LANES), 0)
    for p in range(patches):
        stiff_high[p], stiff_low[p] = split(viscous_step * stiffness[patch_of(p), :])
        multiplicity = jnp.ones((1, width), f32)
        for side in range(2):
            for kind in range(2):
                ahead = jnp.full((1, trace * kind), -1, jnp.int32)
                after = jnp.full((1, LANES - trace * (kind + 1)), -1, jnp.int32)
                points = trace_map[p * 2 + side : p * 2 + side + 1, :]
                slots = jnp.concatenate(([ahead] if kind else []) + [points, after], axis=1)
                one_hot = jnp.where(slots == point, 1.0, 0.0)
                turned = one_hot.T
                pick[p, side, kind] = one_hot.astype(bf16)
                pick_back[p, side, kind] = turned.astype(bf16)
                if kind == 0:
                    gain = near_count[side] if p == edge_patch[side] else 1.0
                    multiplicity += gain * jnp.sum(turned, axis=0, keepdims=True)
        weight[:, patch_of(p)] = relaxation / (multiplicity * multiplicity)
    for p in range(patches - 1):
        across[p, 0] = dot(pick[p, 1, 0], pick_back[p + 1, 0, 0]).astype(bf16)
        across[p, 1] = dot(pick[p + 1, 0, 0], pick_back[p, 1, 0]).astype(bf16)
    number = lax.broadcasted_iota(jnp.int32, (rows, 1), 0) // 8 + me * modes
    rate = 4.0 * number.astype(f32) / (modes * ranks)
    damped[...] = (1.0 + viscous_step * rate * rate) * mass[...]

    def advect_send():
        for offset in range(1, ranks):
            coef_copy(offset).wait_recv()
        own_coef().wait()
        each = 2 * modes * ranks
        fields = coef[...].reshape(3 * each, share)
        high, low = split(fields)
        slopes = dot(high, plane[0]) + dot(low, plane[0]) + dot(high, plane[1])
        xi, eta = slopes[:, :share], slopes[:, share:]
        mine = points_of(me)
        grad_x = metric_main[0:1, mine] * xi + metric_cross[0:1, mine] * eta
        grad_y = metric_cross[1:2, mine] * xi + metric_main[1:2, mine] * eta

        def physical(table, values):
            high, low = split(jnp.concatenate(values, axis=1))
            return dot(table, jnp.concatenate([high, high, low], axis=0))

        def part(value, c):
            return value[c * each : (c + 1) * each]

        plain = physical(tables[...], [part(fields, c) for c in range(3)])
        u, v, w = (plain[:NZ, c * share : (c + 1) * share] for c in range(3))
        for c in range(3):
            slope = physical(tables[:NZ], [part(grad_x, c), part(grad_y, c)])
            advection = (
                u * slope[:, :share]
                + v * slope[:, share:]
                + w * plain[NZ:, c * share : (c + 1) * share]
            )
            high, low = split(advection)
            total = dot(forward[0], high) + dot(forward[0], low) + dot(forward[1], high)
            hat[pl.ds(2 * c, 2)] = total.reshape(2, modes * ranks, share)
            for offset in range(1, ranks):
                hat_copy(offset, c).start()
        own_hat().start()

    advect_send()

    def prepare(k, carry):
        span = pl.ds(pl.multiple_of(k * trace, trace), trace)
        for p in range(patches):
            pltpu.make_async_copy(
                precond.at[k, patch_of(p), :], raw.at[k, patch_of(p), :], raw_sem.at[k, p]
            ).wait()
            block = raw[k, patch_of(p), :]
            high, low = split(block.T)
            inverse_high[k, p] = high
            inverse_low[k, p] = low
            plain_high, plain_low = split(block)
            for side in range(2):
                if p == edge_patch[side]:
                    choose = pick_back[p, side, 0, :trace, :]
                    edge_high[side, span, :] = dot(choose, high).astype(bf16)
                    edge_low[side, span, :] = dot(choose, low).astype(bf16)
                    rows_high[side, span, :] = dot(choose, plain_high)
                    rows_low[side, span, :] = dot(choose, plain_low)
        return carry

    lax.fori_loop(0, modes, prepare, 0)
    for side in range(2):
        choose = pick[edge_patch[side], side, 1]
        corner_out[side] = dot(edge_high[side], choose) + dot(edge_low[side], choose)

        @pl.when(has[side])
        def _():
            corner_copy(side).start()
    for side in range(2):
        gate_high[side, :, :wide] = rows_high[side].T.astype(bf16)
        gate_high[side, :, wide:] = pick[edge_patch[side], side, 0]
        gate_low[side] = rows_low[side].T.astype(bf16)
        inward = across[0 if side == 0 else patches - 2, side]
        beyond_high[side] = dot(edge_high[side], inward).astype(bf16)
        beyond_low[side] = dot(edge_low[side], inward).astype(bf16)
    for side in range(2):
        @pl.when(has[side])
        def _():
            corner_wait(side)
        corner_high[side], corner_low[side] = split(corner_in[side])

    lane = lax.broadcasted_iota(jnp.int32, (rows, LANES), 1)
    block_mask = (
        lax.broadcasted_iota(jnp.int32, (rows, wide), 0) // 8
        == lax.broadcasted_iota(jnp.int32, (rows, wide), 1) // trace
    )

    def repeated(value):
        total = value
        for turn in range(1, LANES // trace):
            total = total + pltpu.roll(value, turn * trace, 1)
        return total

    def spread(note):
        total = repeated(jnp.where(lane < trace, note, 0.0))
        tiled = jnp.concatenate([total] * (wide // LANES), axis=1)
        return jnp.where(block_mask, tiled, 0.0)

    def noted(parts, side):
        sent = folded(dot(parts, gate_high[side]))
        traced = sent[:, :wide] + folded(dot(parts, gate_low[side]))
        traced = jnp.where(block_mask, traced, 0.0)
        total = traced[:, :LANES]
        for start in range(LANES, wide, LANES):
            total = total + traced[:, start : start + LANES]
        return sent[:, wide:] + jnp.where(lane >= trace, repeated(total), 0.0)

    def advect_receive():
        for offset in range(1, ranks):
            coef_copy(offset).wait_send()
            for c in range(3):
                hat_copy(offset, c).wait_recv()
        own_hat().wait()
        for offset in range(1, ranks):
            for c in range(3):
                hat_copy(offset, c).wait_send()
        source = (state[...] - time_step * returned[...]).reshape(6 * modes, patches * width)
        local[...] = mass[...] * reordered(move[...], source)

    def assembled(parts):
        result = list(parts)
        for p in range(patches - 1):
            result[p + 1] = result[p + 1] + moved(parts[p], across[p, 0])
            result[p] = result[p] + moved(parts[p + 1], across[p, 1])
        return result

    def sweep(number, first):
        slot = lax.rem(number, 2)
        terms = []
        for p in range(patches):
            term = local[:, patch_of(p)]
            if not first:
                value = iterate[:, patch_of(p)]
                term = (
                    term
                    - product(value, stiff_high[p], stiff_low[p])
                    - damped[:, patch_of(p)] * value
                )
            terms.append(term)
        lines = [both(term) for term in assembled(terms)]

        def corrected(p, k):
            line = lines[p][k * 16 : (k + 1) * 16]
            return dot(line, inverse_high[k, p]) + dot(line, inverse_low[k, p])

        blocks = [(p, k) for p in range(patches) for k in range(modes)]
        early, late = len(blocks) // 4, len(blocks) - len(blocks) // 4
        found = {}
        notes = [noted(lines[edge_patch[side]], side) for side in range(2)]
        for side in range(2):
            note_out[side] = notes[side]
        for block in blocks[:early]:
            found[block] = corrected(*block)
        for side in range(2):
            @pl.when(has[side])
            def _():
                note_copy(side, slot).start()
        for block in blocks[early:late]:
            found[block] = corrected(*block)
        near = [product(spread(notes[side]), corner_high[side], corner_low[side]) for side in range(2)]
        for side in range(2):
            @pl.when(has[side])
            def _():
                note_wait(side, slot)
        gains = [jnp.zeros((rows, width), f32)] * patches
        for side in range(2):
            p, inner = edge_patch[side], edge_patch[side] + 1 - 2 * side
            note = note_in[slot, side]
            spread_note = both(spread(note))
            gains[p] = gains[p] + folded(
                dot(spread_note, edge_high[side])
                + dot(spread_note, edge_low[side])
                + dot(both(note + near[side]), pick_back[p, side, 1])
            )
            gains[inner] = gains[inner] + folded(
                dot(spread_note, beyond_high[side]) + dot(spread_note, beyond_low[side])
            )
        for block in blocks[late:]:
            found[block] = corrected(*block)
        parts = [
            folded(jnp.concatenate([found[p, k] for k in range(modes)], axis=0))
            for p in range(patches)
        ]
        total = assembled(parts)
        for p in range(patches):
            step = weight[:, patch_of(p)] * (total[p] + gains[p])
            iterate[:, patch_of(p)] = step if first else iterate[:, patch_of(p)] + step

    def later_sweep(number, carry):
        sweep(number, False)
        return carry

    def level(number, carry):
        advect_receive()
        sweep(0, True)
        lax.fori_loop(1, ITERS, later_sweep, 0)
        state[...] = reordered(back[...], iterate[...]).reshape(6, modes, patches * width)

        @pl.when(number < STEPS - 1)
        def _():
            send_coef()
            advect_send()

        return carry

    lax.fori_loop(0, STEPS, level, 0)
    out[...] = exactly(leave[...], iterate[...]).reshape(3, 2 * modes, patches * width)


def on_device(velocity, metric_main, metric_cross, stiffness, mass, precond, trace_map):
    ranks, depth = lax.axis_size("mode"), lax.axis_size("elem")
    rows, points = velocity.shape[1:]
    modes = rows // 2
    patches, _, trace = trace_map.shape
    width = stiffness.shape[1]
    share = points // ranks
    if modes % 8 or share != LANES or LANES % trace or (modes * trace) % LANES or patches < 2:
        return general_device(
            velocity, metric_main, metric_cross, stiffness, mass, precond, trace_map
        )
    basis, slope, forward = spanwise_tables(modes * ranks)
    vmem = pl.BlockSpec(memory_space=pltpu.VMEM)
    wide = modes * trace
    blocks = (modes, patches, width, width)
    return pl.pallas_call(
        functools.partial(kernel, ranks, depth, modes, patches, width, trace, share),
        out_shape=jax.ShapeDtypeStruct(velocity.shape, f32),
        in_specs=[vmem] * 13 + [pl.BlockSpec(memory_space=pl.ANY)],
        out_specs=vmem,
        scratch_shapes=[
            pltpu.VMEM((modes, patches * width, width), f32),
            pltpu.VMEM(blocks, bf16),
            pltpu.VMEM(blocks, bf16),
            pltpu.VMEM((patches, width, width), bf16),
            pltpu.VMEM((patches, width, width), bf16),
            pltpu.VMEM((patches - 1, 2, width, width), bf16),
            pltpu.VMEM((2, wide, width), bf16),
            pltpu.VMEM((2, wide, width), bf16),
            pltpu.VMEM((2, wide, width), bf16),
            pltpu.VMEM((2, wide, width), bf16),
            pltpu.VMEM((2, wide, width), f32),
            pltpu.VMEM((2, wide, width), f32),
            pltpu.VMEM((2, width, wide + LANES), bf16),
            pltpu.VMEM((2, width, wide), bf16),
            pltpu.VMEM((patches, 2, 2, width, LANES), bf16),
            pltpu.VMEM((patches, 2, 2, LANES, width), bf16),
            pltpu.VMEM((2, wide, LANES), f32),
            pltpu.VMEM((2, wide, LANES), f32),
            pltpu.VMEM((2, wide, LANES), bf16),
            pltpu.VMEM((2, wide, LANES), bf16),
            pltpu.VMEM((6, modes, points), f32),
            pltpu.VMEM((6, modes * ranks, share), f32),
            pltpu.VMEM((6, modes * ranks, share), f32),
            pltpu.VMEM((6, modes, points), f32),
            pltpu.VMEM((8 * modes, points), f32),
            pltpu.VMEM((8 * modes, points), f32),
            pltpu.VMEM((1, points), f32),
            pltpu.VMEM((8 * modes, points), f32),
            pltpu.VMEM((2, 8 * modes, LANES), f32),
            pltpu.VMEM((2, 2, 8 * modes, LANES), f32),
            pltpu.SemaphoreType.DMA((modes, patches)),
            pltpu.SemaphoreType.DMA((2,)),
            pltpu.SemaphoreType.DMA((ranks,)),
            pltpu.SemaphoreType.DMA((3, ranks)),
            pltpu.SemaphoreType.DMA((ranks,)),
            pltpu.SemaphoreType.DMA((3, ranks)),
            pltpu.SemaphoreType.DMA((2,)),
            pltpu.SemaphoreType.DMA((2, 2)),
            pltpu.SemaphoreType.DMA((2,)),
            pltpu.SemaphoreType.DMA((2,)),
        ],
        compiler_params=pltpu.CompilerParams(
            collective_id=0, has_side_effects=True, vmem_limit_bytes=56 * 1024 * 1024
        ),
    )(
        velocity,
        metric_main,
        metric_cross,
        stiffness,
        mass.reshape(1, points),
        trace_map.reshape(patches * 2, trace),
        jnp.asarray(np.concatenate([basis, slope], axis=0)),
        jnp.asarray(forward),
        jnp.asarray(plane_tables()),
        *[jnp.asarray(table) for table in row_order(modes)],
        precond,
    )


def shifted(value, axis, steps):
    count = lax.axis_size(axis)
    initial, last = (max(0, -steps), min(count, count - steps))
    return lax.ppermute(value, axis, [(source, source + steps) for source in range(initial, last)])


def general_spanwise():
    spanwise = jnp.arange(NZ, dtype=jnp.int32)
    row_numbers = jnp.arange(KZ, dtype=jnp.int32)
    wavenumber = row_numbers // 2
    product = spanwise[:, None] * wavenumber[None, :] % NZ
    phase_angle = 2.0 * math.pi / NZ * product.astype(jnp.float32)
    is_sine = (row_numbers % 2 == 1)[None, :]
    basis_table = jnp.where(is_sine, jnp.sin(phase_angle), jnp.cos(phase_angle))
    wave_rate = 4.0 * wavenumber.astype(jnp.float32) / MODES
    slope_table = jnp.where(
        is_sine,
        wave_rate[None, :] * jnp.cos(phase_angle),
        -wave_rate[None, :] * jnp.sin(phase_angle),
    )
    norm_factor = jnp.where(row_numbers == 0, 1.0 / NZ, 2.0 / NZ).astype(jnp.float32)
    forward = basis_table.T * norm_factor[:, None]
    return (basis_table, slope_table, forward, wave_rate)


def general_plane(chebyshev):
    position = jnp.arange(128, dtype=jnp.int32)
    node_column = position % 8
    node_row = position // 8 % 8
    element = position // 64
    eight = jnp.arange(8, dtype=jnp.int32)[None, :]
    pick_column = (node_column[:, None] == eight).astype(jnp.float32)
    pick_row = (node_row[:, None] == eight).astype(jnp.float32)
    same_element = element[:, None] == element[None, :]
    along_xi = jnp.dot(
        jnp.dot(pick_column, chebyshev.T, precision=highest_precision),
        pick_column.T,
        precision=highest_precision,
    )
    along_eta = jnp.dot(
        jnp.dot(pick_row, chebyshev.T, precision=highest_precision),
        pick_row.T,
        precision=highest_precision,
    )
    xi_table = jnp.where(same_element & (node_row[:, None] == node_row[None, :]), along_xi, 0.0)
    eta_table = jnp.where(
        same_element & (node_column[:, None] == node_column[None, :]), along_eta, 0.0
    )
    return (xi_table, eta_table)


def plane_slopes(values, xi_table, eta_table, main_part, cross_part):
    flat_values = values.reshape(-1, 128)
    xi_slope = jnp.dot(flat_values, xi_table, precision=highest_precision).reshape(values.shape)
    eta_slope = jnp.dot(flat_values, eta_table, precision=highest_precision).reshape(values.shape)
    grad_x = main_part[0] * xi_slope + cross_part[0] * eta_slope
    grad_y = cross_part[1] * xi_slope + main_part[1] * eta_slope
    return (grad_x, grad_y)


def general_device(velocity, metric_main, metric_cross, stiffness, mass, precond, trace_map):
    rows_dev = velocity.shape[1]
    points = velocity.shape[2]
    patch_dev = trace_map.shape[0]
    width = stiffness.shape[1]
    trace_width = trace_map.shape[2]
    modes_dev = rows_dev // 2
    chebyshev = jnp.asarray(chebyshev_matrix(), jnp.float32)
    xi_table, eta_table = general_plane(chebyshev)
    basis_table, slope_table, forward, wave_all = general_spanwise()
    wave_rows = lax.dynamic_slice_in_dim(wave_all, lax.axis_index("mode") * rows_dev, rows_dev)
    damping = (1.0 + viscous_step * wave_rows * wave_rows)[None, :, None, None]
    patches = stiffness.reshape(patch_dev, width, width)
    inverse = precond.reshape(modes_dev, patch_dev, width, width)
    patch_mass = mass.reshape(patch_dev, width)
    point_numbers = jnp.arange(width, dtype=jnp.int32)[None, None, :]
    left_pick = (trace_map[:, 0][:, :, None] == point_numbers).astype(jnp.float32)
    right_pick = (trace_map[:, 1][:, :, None] == point_numbers).astype(jnp.float32)
    global_patch = lax.axis_index("elem") * patch_dev + jnp.arange(patch_dev)
    last_patch = patch_dev * lax.axis_size("elem") - 1
    left_gain = (global_patch > 0).astype(jnp.float32)[:, None]
    right_gain = (global_patch < last_patch).astype(jnp.float32)[:, None]
    multiplicity = (
        1.0 + left_gain * jnp.sum(left_pick, axis=1) + right_gain * jnp.sum(right_pick, axis=1)
    )
    weight = relaxation / (multiplicity * multiplicity)
    share = points // lax.axis_size("mode")
    main_share = lax.dynamic_slice_in_dim(metric_main, lax.axis_index("mode") * share, share, 1)
    cross_share = lax.dynamic_slice_in_dim(metric_cross, lax.axis_index("mode") * share, share, 1)

    def assemble(values):
        left_values = jnp.einsum("crpl,pjl->crpj", values, left_pick, precision=highest_precision)
        right_values = jnp.einsum("crpl,pjl->crpj", values, right_pick, precision=highest_precision)
        upward = shifted(right_values[:, :, -1].reshape(-1), "elem", 1)
        downward = shifted(left_values[:, :, 0].reshape(-1), "elem", -1)
        from_below = jnp.concatenate(
            [upward.reshape(3, rows_dev, 1, trace_width), right_values[:, :, :-1]], axis=2
        )
        from_above = jnp.concatenate(
            [left_values[:, :, 1:], downward.reshape(3, rows_dev, 1, trace_width)], axis=2
        )
        below_points = jnp.einsum(
            "crpj,pjl->crpl", from_below, left_pick, precision=highest_precision
        )
        above_points = jnp.einsum(
            "crpj,pjl->crpl", from_above, right_pick, precision=highest_precision
        )
        return values + below_points + above_points

    state = velocity
    for time_level in range(STEPS):
        coefficients = lax.all_to_all(state, "mode", split_axis=2, concat_axis=1, tiled=True)
        grad_x, grad_y = plane_slopes(coefficients, xi_table, eta_table, main_share, cross_share)
        plane_part = jnp.einsum(
            "frp,zr->fpz",
            jnp.concatenate([coefficients, grad_x, grad_y], axis=0),
            basis_table,
            precision=highest_precision,
        )
        spanwise_part = jnp.einsum(
            "frp,zr->fpz", coefficients, slope_table, precision=highest_precision
        )
        physical = jnp.concatenate([plane_part, spanwise_part], axis=0)
        advection = (
            physical[0:1] * physical[3:6]
            + physical[1:2] * physical[6:9]
            + physical[2:3] * physical[9:12]
        )
        advection_points = jnp.einsum(
            "ipz,rz->irp", advection, forward, precision=highest_precision
        )
        advection_hat = lax.all_to_all(
            advection_points, "mode", split_axis=1, concat_axis=2, tiled=True
        )
        source = (state - time_step * advection_hat).reshape(3, rows_dev, patch_dev, width)
        local_term = patch_mass * source
        iterate = jnp.zeros_like(source)
        for sweep_number in range(ITERS):
            if sweep_number == 0:
                residual = assemble(local_term)
            else:
                stiff_part = jnp.einsum(
                    "pij,crpj->crpi", patches, iterate, precision=highest_precision
                )
                residual = assemble(
                    local_term - viscous_step * stiff_part - damping * patch_mass * iterate
                )
            grouped = residual.reshape(3, modes_dev, 2, patch_dev, width)
            correction = jnp.einsum(
                "kpij,ckhpj->ckhpi", inverse, grouped, precision=highest_precision
            ).reshape(3, rows_dev, patch_dev, width)
            iterate = iterate + weight * assemble(correction)
        state = iterate.reshape(3, rows_dev, points)
    return state


def solution(mesh):
    return jax.shard_map(
        on_device,
        mesh=mesh,
        in_specs=(
            P(None, "mode", "elem"),
            P(None, "elem"),
            P(None, "elem"),
            P("elem", None),
            P("elem"),
            P("mode", "elem", None),
            P("elem", None, None),
        ),
        out_specs=P(None, "mode", "elem"),
        check_vma=False,
    )
```

```python
import functools
import math

import jax
import jax.numpy as jnp
import numpy as np
from jax import lax
from jax.experimental import pallas as pl
from jax.experimental.pallas import tpu as pltpu
from jax.sharding import PartitionSpec as P

NZ = 256
STEPS = 4
ITERS = 4
LANES = 128

viscous_step = 0.5
time_step = 0.02
relaxation = 0.8
f32 = jnp.float32
bf16 = jnp.bfloat16
MODES = 64
KZ = 128
highest_precision = lax.Precision.HIGHEST


def chebyshev_matrix():
    node_points = np.cos(np.pi * np.arange(8) / 7.0)
    weights = np.where((np.arange(8) == 0) | (np.arange(8) == 7), 2.0, 1.0)
    parity = np.where((np.arange(8)[:, None] + np.arange(8)[None, :]) % 2 == 0, 1.0, -1.0)
    identity = np.eye(8)
    spacing = node_points[:, None] - node_points[None, :] + identity
    off_diagonal = weights[:, None] / weights[None, :] * parity / spacing * (1.0 - identity)
    return off_diagonal - identity * off_diagonal.sum(axis=1)[:, None]


def pair(table):
    table = np.asarray(table, np.float32)
    high = table.astype(bf16)
    low = (table - high.astype(np.float32)).astype(bf16)
    return high, low


def spanwise_tables(modes):
    angle = 2.0 * math.pi / NZ * (np.arange(NZ)[:, None] * np.arange(modes)[None, :] % NZ)
    rate = 4.0 * np.arange(modes) / modes
    cosine, sine = np.cos(angle), np.sin(angle)
    basis = np.concatenate([cosine, sine], axis=1)
    slope = np.concatenate([-rate * sine, rate * cosine], axis=1)
    factor = np.full(2 * modes, 2.0 / NZ)
    factor[0] = 1.0 / NZ
    forward = basis.T * factor[:, None]

    def left_three(table):
        high, low = pair(table)
        return np.concatenate([high, low, high], axis=1)

    return left_three(basis), left_three(slope), np.stack(pair(forward))


def plane_tables():
    chebyshev = chebyshev_matrix()
    position = np.arange(LANES)
    column, row, element = position % 8, position // 8 % 8, position // 64
    same = element[:, None] == element[None, :]
    xi = np.where(same & (row[:, None] == row[None, :]), chebyshev.T[column][:, column], 0.0)
    eta = np.where(same & (column[:, None] == column[None, :]), chebyshev.T[row][:, row], 0.0)
    return np.stack(pair(np.concatenate([xi, eta], axis=1)))


def row_order(modes):
    move = np.zeros((modes * 8, 6 * modes), np.float32)
    for field in range(6):
        for mode in range(modes):
            move[mode * 8 + field, field * modes + mode] = 1.0
    shuffle = np.zeros((6 * modes, 6 * modes), np.float32)
    for c in range(3):
        for half in range(2):
            for mode in range(modes):
                shuffle[(2 * c + half) * modes + mode, (c * modes + mode) * 2 + half] = 1.0
    return [table.astype(bf16) for table in (move, move.T, shuffle, shuffle.T @ move.T)]


def dot(a, b):
    return lax.dot_general(a, b, (((1,), (0,)), ((), ())), preferred_element_type=f32)


def split(value):
    high = value.astype(bf16)
    return high, (value - high.astype(f32)).astype(bf16)


def both(value):
    high = value.astype(bf16).astype(f32)
    low = value - high
    tiles = []
    for start in range(0, value.shape[0], 8):
        tiles += [high[start : start + 8], low[start : start + 8]]
    return jnp.concatenate(tiles, axis=0).astype(bf16)


def folded(value):
    tiles = [
        value[start : start + 8] + value[start + 8 : start + 16]
        for start in range(0, value.shape[0], 16)
    ]
    return jnp.concatenate(tiles, axis=0)


def product(value, high, low):
    parts = both(value)
    return folded(dot(parts, high) + dot(parts, low))


def moved(value, one_hot):
    return folded(dot(both(value), one_hot))


def reordered(move, value):
    high, low = split(value)
    return dot(move, high) + dot(move, low)


def exactly(move, value):
    high, low = split(value)
    rest = (value - high.astype(f32) - low.astype(f32)).astype(bf16)
    return dot(move, high) + (dot(move, low) + dot(move, rest))


def kernel(
    ranks,
    depth,
    modes,
    patches,
    width,
    trace,
    share,
    velocity,
    metric_main,
    metric_cross,
    stiffness,
    mass,
    trace_map,
    tables,
    forward,
    plane,
    move,
    back,
    enter,
    leave,
    precond,
    out,
    raw,
    inverse_high,
    inverse_low,
    stiff_high,
    stiff_low,
    across,
    edge_high,
    edge_low,
    beyond_high,
    beyond_low,
    rows_high,
    rows_low,
    gate_high,
    gate_low,
    pick,
    pick_back,
    corner_out,
    corner_in,
    corner_high,
    corner_low,
    state,
    coef,
    hat,
    returned,
    local,
    damped,
    weight,
    iterate,
    note_out,
    note_in,
    raw_sem,
    own_sem,
    coef_send,
    hat_send,
    coef_sem,
    hat_sem,
    note_send,
    note_recv,
    corner_send,
    corner_recv,
):
    me = lax.axis_index("mode")
    place = lax.axis_index("elem")
    has = (place > 0, place < depth - 1)
    beside = (place - 1, place + 1)
    rows = 8 * modes
    wide = modes * trace

    def patch_of(p):
        return pl.ds(p * width, width)

    for k in range(modes):
        for p in range(patches):
            pltpu.make_async_copy(
                precond.at[k, patch_of(p), :], raw.at[k, patch_of(p), :], raw_sem.at[k, p]
            ).start()

    note_in[...] = jnp.zeros_like(note_in)
    corner_in[...] = jnp.zeros_like(corner_in)
    state[...] = exactly(enter[...], velocity[...].reshape(6 * modes, patches * width)).reshape(
        6, modes, patches * width
    )

    barrier = pltpu.get_barrier_semaphore()
    for offset in range(1, ranks):
        pl.semaphore_signal(
            barrier, 1, device_id={"mode": lax.rem(me + offset, ranks)},
            device_id_type=pl.DeviceIdType.MESH,
        )
    for side in range(2):
        @pl.when(has[side])
        def _():
            pl.semaphore_signal(
                barrier, 1, device_id={"elem": beside[side]}, device_id_type=pl.DeviceIdType.MESH
            )
    near_side = (jnp.minimum(place, 1), jnp.minimum(depth - 1 - place, 1))
    near_count = [side.astype(f32) for side in near_side]
    pl.semaphore_wait(barrier, ranks - 1 + near_side[0] + near_side[1])

    def points_of(rank):
        return pl.ds(pl.multiple_of(rank * share, share), share)

    def modes_of(rank):
        return pl.ds(pl.multiple_of(rank * modes, modes), modes)

    def coef_copy(offset):
        to = lax.rem(me + offset, ranks)
        return pltpu.make_async_remote_copy(
            src_ref=state.at[:, :, points_of(to)],
            dst_ref=coef.at[:, modes_of(me), :],
            send_sem=coef_send.at[offset],
            recv_sem=coef_sem.at[offset],
            device_id={"mode": to},
            device_id_type=pl.DeviceIdType.MESH,
        )

    def hat_copy(offset, c):
        to = lax.rem(me + offset, ranks)
        return pltpu.make_async_remote_copy(
            src_ref=hat.at[pl.ds(2 * c, 2), modes_of(to), :],
            dst_ref=returned.at[pl.ds(2 * c, 2), :, points_of(me)],
            send_sem=hat_send.at[c, offset],
            recv_sem=hat_sem.at[c, offset],
            device_id={"mode": to},
            device_id_type=pl.DeviceIdType.MESH,
        )

    def own_coef():
        return pltpu.make_async_copy(
            state.at[:, :, points_of(me)], coef.at[:, modes_of(me), :], own_sem.at[0]
        )

    def own_hat():
        return pltpu.make_async_copy(
            hat.at[:, modes_of(me), :], returned.at[:, :, points_of(me)], own_sem.at[1]
        )

    def send_coef():
        for offset in range(1, ranks):
            coef_copy(offset).start()
        own_coef().start()

    def note_copy(side, slot):
        return pltpu.make_async_remote_copy(
            src_ref=note_out.at[side],
            dst_ref=note_in.at[slot, 1 - side],
            send_sem=note_send.at[side],
            recv_sem=note_recv.at[slot, 1 - side],
            device_id={"elem": beside[side]},
            device_id_type=pl.DeviceIdType.MESH,
        )

    def corner_copy(side):
        return pltpu.make_async_remote_copy(
            src_ref=corner_out.at[side],
            dst_ref=corner_in.at[1 - side],
            send_sem=corner_send.at[side],
            recv_sem=corner_recv.at[1 - side],
            device_id={"elem": beside[side]},
            device_id_type=pl.DeviceIdType.MESH,
        )

    def note_wait(side, slot):
        note_copy(side, slot).wait_send()
        pltpu.make_async_remote_copy(
            src_ref=note_out.at[side],
            dst_ref=note_in.at[slot, side],
            send_sem=note_send.at[side],
            recv_sem=note_recv.at[slot, side],
            device_id={"elem": beside[side]},
            device_id_type=pl.DeviceIdType.MESH,
        ).wait_recv()

    def corner_wait(side):
        corner_copy(side).wait_send()
        pltpu.make_async_remote_copy(
            src_ref=corner_out.at[side],
            dst_ref=corner_in.at[side],
            send_sem=corner_send.at[side],
            recv_sem=corner_recv.at[side],
            device_id={"elem": beside[side]},
            device_id_type=pl.DeviceIdType.MESH,
        ).wait_recv()

    send_coef()

    edge_patch = (0, patches - 1)
    point = lax.broadcasted_iota(jnp.int32, (width, LANES), 0)
    for p in range(patches):
        stiff_high[p], stiff_low[p] = split(viscous_step * stiffness[patch_of(p), :])
        multiplicity = jnp.ones((1, width), f32)
        for side in range(2):
            for kind in range(2):
                ahead = jnp.full((1, trace * kind), -1, jnp.int32)
                after = jnp.full((1, LANES - trace * (kind + 1)), -1, jnp.int32)
                points = trace_map[p * 2 + side : p * 2 + side + 1, :]
                slots = jnp.concatenate(([ahead] if kind else []) + [points, after], axis=1)
                one_hot = jnp.where(slots == point, 1.0, 0.0)
                turned = one_hot.T
                pick[p, side, kind] = one_hot.astype(bf16)
                pick_back[p, side, kind] = turned.astype(bf16)
                if kind == 0:
                    gain = near_count[side] if p == edge_patch[side] else 1.0
                    multiplicity += gain * jnp.sum(turned, axis=0, keepdims=True)
        weight[:, patch_of(p)] = relaxation / (multiplicity * multiplicity)
    for p in range(patches - 1):
        across[p, 0] = dot(pick[p, 1, 0], pick_back[p + 1, 0, 0]).astype(bf16)
        across[p, 1] = dot(pick[p + 1, 0, 0], pick_back[p, 1, 0]).astype(bf16)
    number = lax.broadcasted_iota(jnp.int32, (rows, 1), 0) // 8 + me * modes
    rate = 4.0 * number.astype(f32) / (modes * ranks)
    damped[...] = (1.0 + viscous_step * rate * rate) * mass[...]

    def advect_send():
        for offset in range(1, ranks):
            coef_copy(offset).wait_recv()
        own_coef().wait()
        each = 2 * modes * ranks
        fields = coef[...].reshape(3 * each, share)
        high, low = split(fields)
        slopes = dot(high, plane[0]) + dot(low, plane[0]) + dot(high, plane[1])
        xi, eta = slopes[:, :share], slopes[:, share:]
        mine = points_of(me)
        grad_x = metric_main[0:1, mine] * xi + metric_cross[0:1, mine] * eta
        grad_y = metric_cross[1:2, mine] * xi + metric_main[1:2, mine] * eta

        def physical(table, values):
            high, low = split(jnp.concatenate(values, axis=1))
            return dot(table, jnp.concatenate([high, high, low], axis=0))

        def part(value, c):
            return value[c * each : (c + 1) * each]

        plain = physical(tables[...], [part(fields, c) for c in range(3)])
        u, v, w = (plain[:NZ, c * share : (c + 1) * share] for c in range(3))
        for c in range(3):
            slope = physical(tables[:NZ], [part(grad_x, c), part(grad_y, c)])
            advection = (
                u * slope[:, :share]
                + v * slope[:, share:]
                + w * plain[NZ:, c * share : (c + 1) * share]
            )
            high, low = split(advection)
            total = dot(forward[0], high) + dot(forward[0], low) + dot(forward[1], high)
            hat[pl.ds(2 * c, 2)] = total.reshape(2, modes * ranks, share)
            for offset in range(1, ranks):
                hat_copy(offset, c).start()
        own_hat().start()

    advect_send()

    def prepare(k, carry):
        span = pl.ds(pl.multiple_of(k * trace, trace), trace)
        for p in range(patches):
            pltpu.make_async_copy(
                precond.at[k, patch_of(p), :], raw.at[k, patch_of(p), :], raw_sem.at[k, p]
            ).wait()
            block = raw[k, patch_of(p), :]
            high, low = split(block.T)
            inverse_high[k, p] = high
            inverse_low[k, p] = low
            plain_high, plain_low = split(block)
            for side in range(2):
                if p == edge_patch[side]:
                    choose = pick_back[p, side, 0, :trace, :]
                    edge_high[side, span, :] = dot(choose, high).astype(bf16)
                    edge_low[side, span, :] = dot(choose, low).astype(bf16)
                    rows_high[side, span, :] = dot(choose, plain_high)
                    rows_low[side, span, :] = dot(choose, plain_low)
        return carry

    lax.fori_loop(0, modes, prepare, 0)
    for side in range(2):
        choose = pick[edge_patch[side], side, 1]
        corner_out[side] = dot(edge_high[side], choose) + dot(edge_low[side], choose)

        @pl.when(has[side])
        def _():
            corner_copy(side).start()
    for side in range(2):
        gate_high[side, :, :wide] = rows_high[side].T.astype(bf16)
        gate_high[side, :, wide:] = pick[edge_patch[side], side, 0]
        gate_low[side] = rows_low[side].T.astype(bf16)
        inward = across[0 if side == 0 else patches - 2, side]
        beyond_high[side] = dot(edge_high[side], inward).astype(bf16)
        beyond_low[side] = dot(edge_low[side], inward).astype(bf16)
    for side in range(2):
        @pl.when(has[side])
        def _():
            corner_wait(side)
        corner_high[side], corner_low[side] = split(corner_in[side])

    lane = lax.broadcasted_iota(jnp.int32, (rows, LANES), 1)
    block_mask = (
        lax.broadcasted_iota(jnp.int32, (rows, wide), 0) // 8
        == lax.broadcasted_iota(jnp.int32, (rows, wide), 1) // trace
    )

    def packed(note):
        half = rows // 2
        return jnp.where(
            lane[:half] < LANES // 2, note[:half], pltpu.roll(note[half:], LANES // 2, 1)
        )

    def unpacked(note):
        return jnp.concatenate([note, pltpu.roll(note, LANES // 2, 1)], axis=0)

    def repeated(value):
        total = value
        for turn in range(1, LANES // trace):
            total = total + pltpu.roll(value, turn * trace, 1)
        return total

    def spread(note):
        total = repeated(jnp.where(lane < trace, note, 0.0))
        tiled = jnp.concatenate([total] * (wide // LANES), axis=1)
        return jnp.where(block_mask, tiled, 0.0)

    def noted(parts, side):
        sent = folded(dot(parts, gate_high[side]))
        traced = sent[:, :wide] + folded(dot(parts, gate_low[side]))
        traced = jnp.where(block_mask, traced, 0.0)
        total = traced[:, :LANES]
        for start in range(LANES, wide, LANES):
            total = total + traced[:, start : start + LANES]
        return sent[:, wide:] + jnp.where(lane >= trace, repeated(total), 0.0)

    def advect_receive():
        for offset in range(1, ranks):
            coef_copy(offset).wait_send()
            for c in range(3):
                hat_copy(offset, c).wait_recv()
        own_hat().wait()
        for offset in range(1, ranks):
            for c in range(3):
                hat_copy(offset, c).wait_send()
        source = (state[...] - time_step * returned[...]).reshape(6 * modes, patches * width)
        local[...] = mass[...] * reordered(move[...], source)

    def assembled(parts):
        result = list(parts)
        for p in range(patches - 1):
            result[p + 1] = result[p + 1] + moved(parts[p], across[p, 0])
            result[p] = result[p] + moved(parts[p + 1], across[p, 1])
        return result

    def sweep(number, first):
        slot = lax.rem(number, 2)
        terms = []
        for p in range(patches):
            term = local[:, patch_of(p)]
            if not first:
                value = iterate[:, patch_of(p)]
                term = (
                    term
                    - product(value, stiff_high[p], stiff_low[p])
                    - damped[:, patch_of(p)] * value
                )
            terms.append(term)
        lines = [both(term) for term in assembled(terms)]

        def corrected(p, k):
            line = lines[p][k * 16 : (k + 1) * 16]
            return dot(line, inverse_high[k, p]) + dot(line, inverse_low[k, p])

        notes = [noted(lines[edge_patch[side]], side) for side in range(2)]
        for side in range(2):
            note_out[side] = packed(notes[side])
        for side in range(2):
            @pl.when(has[side])
            def _():
                note_copy(side, slot).start()
        parts = []
        for p in range(patches):
            found = [corrected(p, k) for k in range(modes)]
            parts.append(folded(jnp.concatenate(found, axis=0)))
        total = assembled(parts)
        near = [product(spread(notes[side]), corner_high[side], corner_low[side]) for side in range(2)]
        for side in range(2):
            @pl.when(has[side])
            def _():
                note_wait(side, slot)
        gains = [jnp.zeros((rows, width), f32)] * patches
        for side in range(2):
            p, inner = edge_patch[side], edge_patch[side] + 1 - 2 * side
            note = unpacked(note_in[slot, side])
            spread_note = both(spread(note))
            gains[p] = gains[p] + folded(
                dot(spread_note, edge_high[side])
                + dot(spread_note, edge_low[side])
                + dot(both(note + near[side]), pick_back[p, side, 1])
            )
            gains[inner] = gains[inner] + folded(
                dot(spread_note, beyond_high[side]) + dot(spread_note, beyond_low[side])
            )
        for p in range(patches):
            step = weight[:, patch_of(p)] * (total[p] + gains[p])
            iterate[:, patch_of(p)] = step if first else iterate[:, patch_of(p)] + step

    def later_sweep(number, carry):
        sweep(number, False)
        return carry

    def level(number, carry):
        advect_receive()
        sweep(0, True)
        lax.fori_loop(1, ITERS, later_sweep, 0)
        state[...] = reordered(back[...], iterate[...]).reshape(6, modes, patches * width)

        @pl.when(number < STEPS - 1)
        def _():
            send_coef()
            advect_send()

        return carry

    lax.fori_loop(0, STEPS, level, 0)
    out[...] = exactly(leave[...], iterate[...]).reshape(3, 2 * modes, patches * width)


def on_device(velocity, metric_main, metric_cross, stiffness, mass, precond, trace_map):
    ranks, depth = lax.axis_size("mode"), lax.axis_size("elem")
    rows, points = velocity.shape[1:]
    modes = rows // 2
    patches, _, trace = trace_map.shape
    width = stiffness.shape[1]
    share = points // ranks
    if modes % 8 or share != LANES or LANES != 4 * trace or (modes * trace) % LANES or patches < 2:
        return general_device(
            velocity, metric_main, metric_cross, stiffness, mass, precond, trace_map
        )
    basis, slope, forward = spanwise_tables(modes * ranks)
    vmem = pl.BlockSpec(memory_space=pltpu.VMEM)
    wide = modes * trace
    blocks = (modes, patches, width, width)
    return pl.pallas_call(
        functools.partial(kernel, ranks, depth, modes, patches, width, trace, share),
        out_shape=jax.ShapeDtypeStruct(velocity.shape, f32),
        in_specs=[vmem] * 13 + [pl.BlockSpec(memory_space=pl.ANY)],
        out_specs=vmem,
        scratch_shapes=[
            pltpu.VMEM((modes, patches * width, width), f32),
            pltpu.VMEM(blocks, bf16),
            pltpu.VMEM(blocks, bf16),
            pltpu.VMEM((patches, width, width), bf16),
            pltpu.VMEM((patches, width, width), bf16),
            pltpu.VMEM((patches - 1, 2, width, width), bf16),
            pltpu.VMEM((2, wide, width), bf16),
            pltpu.VMEM((2, wide, width), bf16),
            pltpu.VMEM((2, wide, width), bf16),
            pltpu.VMEM((2, wide, width), bf16),
            pltpu.VMEM((2, wide, width), f32),
            pltpu.VMEM((2, wide, width), f32),
            pltpu.VMEM((2, width, wide + LANES), bf16),
            pltpu.VMEM((2, width, wide), bf16),
            pltpu.VMEM((patches, 2, 2, width, LANES), bf16),
            pltpu.VMEM((patches, 2, 2, LANES, width), bf16),
            pltpu.VMEM((2, wide, LANES), f32),
            pltpu.VMEM((2, wide, LANES), f32),
            pltpu.VMEM((2, wide, LANES), bf16),
            pltpu.VMEM((2, wide, LANES), bf16),
            pltpu.VMEM((6, modes, points), f32),
            pltpu.VMEM((6, modes * ranks, share), f32),
            pltpu.VMEM((6, modes * ranks, share), f32),
            pltpu.VMEM((6, modes, points), f32),
            pltpu.VMEM((8 * modes, points), f32),
            pltpu.VMEM((8 * modes, points), f32),
            pltpu.VMEM((1, points), f32),
            pltpu.VMEM((8 * modes, points), f32),
            pltpu.VMEM((2, 4 * modes, LANES), f32),
            pltpu.VMEM((2, 2, 4 * modes, LANES), f32),
            pltpu.SemaphoreType.DMA((modes, patches)),
            pltpu.SemaphoreType.DMA((2,)),
            pltpu.SemaphoreType.DMA((ranks,)),
            pltpu.SemaphoreType.DMA((3, ranks)),
            pltpu.SemaphoreType.DMA((ranks,)),
            pltpu.SemaphoreType.DMA((3, ranks)),
            pltpu.SemaphoreType.DMA((2,)),
            pltpu.SemaphoreType.DMA((2, 2)),
            pltpu.SemaphoreType.DMA((2,)),
            pltpu.SemaphoreType.DMA((2,)),
        ],
        compiler_params=pltpu.CompilerParams(
            collective_id=0, has_side_effects=True, vmem_limit_bytes=56 * 1024 * 1024
        ),
    )(
        velocity,
        metric_main,
        metric_cross,
        stiffness,
        mass.reshape(1, points),
        trace_map.reshape(patches * 2, trace),
        jnp.asarray(np.concatenate([basis, slope], axis=0)),
        jnp.asarray(forward),
        jnp.asarray(plane_tables()),
        *[jnp.asarray(table) for table in row_order(modes)],
        precond,
    )


def shifted(value, axis, steps):
    count = lax.axis_size(axis)
    initial, last = (max(0, -steps), min(count, count - steps))
    return lax.ppermute(value, axis, [(source, source + steps) for source in range(initial, last)])


def general_spanwise():
    spanwise = jnp.arange(NZ, dtype=jnp.int32)
    row_numbers = jnp.arange(KZ, dtype=jnp.int32)
    wavenumber = row_numbers // 2
    product = spanwise[:, None] * wavenumber[None, :] % NZ
    phase_angle = 2.0 * math.pi / NZ * product.astype(jnp.float32)
    is_sine = (row_numbers % 2 == 1)[None, :]
    basis_table = jnp.where(is_sine, jnp.sin(phase_angle), jnp.cos(phase_angle))
    wave_rate = 4.0 * wavenumber.astype(jnp.float32) / MODES
    slope_table = jnp.where(
        is_sine,
        wave_rate[None, :] * jnp.cos(phase_angle),
        -wave_rate[None, :] * jnp.sin(phase_angle),
    )
    norm_factor = jnp.where(row_numbers == 0, 1.0 / NZ, 2.0 / NZ).astype(jnp.float32)
    forward = basis_table.T * norm_factor[:, None]
    return (basis_table, slope_table, forward, wave_rate)


def general_plane(chebyshev):
    position = jnp.arange(128, dtype=jnp.int32)
    node_column = position % 8
    node_row = position // 8 % 8
    element = position // 64
    eight = jnp.arange(8, dtype=jnp.int32)[None, :]
    pick_column = (node_column[:, None] == eight).astype(jnp.float32)
    pick_row = (node_row[:, None] == eight).astype(jnp.float32)
    same_element = element[:, None] == element[None, :]
    along_xi = jnp.dot(
        jnp.dot(pick_column, chebyshev.T, precision=highest_precision),
        pick_column.T,
        precision=highest_precision,
    )
    along_eta = jnp.dot(
        jnp.dot(pick_row, chebyshev.T, precision=highest_precision),
        pick_row.T,
        precision=highest_precision,
    )
    xi_table = jnp.where(same_element & (node_row[:, None] == node_row[None, :]), along_xi, 0.0)
    eta_table = jnp.where(
        same_element & (node_column[:, None] == node_column[None, :]), along_eta, 0.0
    )
    return (xi_table, eta_table)


def plane_slopes(values, xi_table, eta_table, main_part, cross_part):
    flat_values = values.reshape(-1, 128)
    xi_slope = jnp.dot(flat_values, xi_table, precision=highest_precision).reshape(values.shape)
    eta_slope = jnp.dot(flat_values, eta_table, precision=highest_precision).reshape(values.shape)
    grad_x = main_part[0] * xi_slope + cross_part[0] * eta_slope
    grad_y = cross_part[1] * xi_slope + main_part[1] * eta_slope
    return (grad_x, grad_y)


def general_device(velocity, metric_main, metric_cross, stiffness, mass, precond, trace_map):
    rows_dev = velocity.shape[1]
    points = velocity.shape[2]
    patch_dev = trace_map.shape[0]
    width = stiffness.shape[1]
    trace_width = trace_map.shape[2]
    modes_dev = rows_dev // 2
    chebyshev = jnp.asarray(chebyshev_matrix(), jnp.float32)
    xi_table, eta_table = general_plane(chebyshev)
    basis_table, slope_table, forward, wave_all = general_spanwise()
    wave_rows = lax.dynamic_slice_in_dim(wave_all, lax.axis_index("mode") * rows_dev, rows_dev)
    damping = (1.0 + viscous_step * wave_rows * wave_rows)[None, :, None, None]
    patches = stiffness.reshape(patch_dev, width, width)
    inverse = precond.reshape(modes_dev, patch_dev, width, width)
    patch_mass = mass.reshape(patch_dev, width)
    point_numbers = jnp.arange(width, dtype=jnp.int32)[None, None, :]
    left_pick = (trace_map[:, 0][:, :, None] == point_numbers).astype(jnp.float32)
    right_pick = (trace_map[:, 1][:, :, None] == point_numbers).astype(jnp.float32)
    global_patch = lax.axis_index("elem") * patch_dev + jnp.arange(patch_dev)
    last_patch = patch_dev * lax.axis_size("elem") - 1
    left_gain = (global_patch > 0).astype(jnp.float32)[:, None]
    right_gain = (global_patch < last_patch).astype(jnp.float32)[:, None]
    multiplicity = (
        1.0 + left_gain * jnp.sum(left_pick, axis=1) + right_gain * jnp.sum(right_pick, axis=1)
    )
    weight = relaxation / (multiplicity * multiplicity)
    share = points // lax.axis_size("mode")
    main_share = lax.dynamic_slice_in_dim(metric_main, lax.axis_index("mode") * share, share, 1)
    cross_share = lax.dynamic_slice_in_dim(metric_cross, lax.axis_index("mode") * share, share, 1)

    def assemble(values):
        left_values = jnp.einsum("crpl,pjl->crpj", values, left_pick, precision=highest_precision)
        right_values = jnp.einsum("crpl,pjl->crpj", values, right_pick, precision=highest_precision)
        upward = shifted(right_values[:, :, -1].reshape(-1), "elem", 1)
        downward = shifted(left_values[:, :, 0].reshape(-1), "elem", -1)
        from_below = jnp.concatenate(
            [upward.reshape(3, rows_dev, 1, trace_width), right_values[:, :, :-1]], axis=2
        )
        from_above = jnp.concatenate(
            [left_values[:, :, 1:], downward.reshape(3, rows_dev, 1, trace_width)], axis=2
        )
        below_points = jnp.einsum(
            "crpj,pjl->crpl", from_below, left_pick, precision=highest_precision
        )
        above_points = jnp.einsum(
            "crpj,pjl->crpl", from_above, right_pick, precision=highest_precision
        )
        return values + below_points + above_points

    state = velocity
    for time_level in range(STEPS):
        coefficients = lax.all_to_all(state, "mode", split_axis=2, concat_axis=1, tiled=True)
        grad_x, grad_y = plane_slopes(coefficients, xi_table, eta_table, main_share, cross_share)
        plane_part = jnp.einsum(
            "frp,zr->fpz",
            jnp.concatenate([coefficients, grad_x, grad_y], axis=0),
            basis_table,
            precision=highest_precision,
        )
        spanwise_part = jnp.einsum(
            "frp,zr->fpz", coefficients, slope_table, precision=highest_precision
        )
        physical = jnp.concatenate([plane_part, spanwise_part], axis=0)
        advection = (
            physical[0:1] * physical[3:6]
            + physical[1:2] * physical[6:9]
            + physical[2:3] * physical[9:12]
        )
        advection_points = jnp.einsum(
            "ipz,rz->irp", advection, forward, precision=highest_precision
        )
        advection_hat = lax.all_to_all(
            advection_points, "mode", split_axis=1, concat_axis=2, tiled=True
        )
        source = (state - time_step * advection_hat).reshape(3, rows_dev, patch_dev, width)
        local_term = patch_mass * source
        iterate = jnp.zeros_like(source)
        for sweep_number in range(ITERS):
            if sweep_number == 0:
                residual = assemble(local_term)
            else:
                stiff_part = jnp.einsum(
                    "pij,crpj->crpi", patches, iterate, precision=highest_precision
                )
                residual = assemble(
                    local_term - viscous_step * stiff_part - damping * patch_mass * iterate
                )
            grouped = residual.reshape(3, modes_dev, 2, patch_dev, width)
            correction = jnp.einsum(
                "kpij,ckhpj->ckhpi", inverse, grouped, precision=highest_precision
            ).reshape(3, rows_dev, patch_dev, width)
            iterate = iterate + weight * assemble(correction)
        state = iterate.reshape(3, rows_dev, points)
    return state


def solution(mesh):
    return jax.shard_map(
        on_device,
        mesh=mesh,
        in_specs=(
            P(None, "mode", "elem"),
            P(None, "elem"),
            P(None, "elem"),
            P("elem", None),
            P("elem"),
            P("mode", "elem", None),
            P("elem", None, None),
        ),
        out_specs=P(None, "mode", "elem"),
        check_vma=False,
    )
```

```python
import functools
import math

import jax
import jax.numpy as jnp
import numpy as np
from jax import lax
from jax.experimental import pallas as pl
from jax.experimental.pallas import tpu as pltpu
from jax.sharding import PartitionSpec as P

NZ = 256
STEPS = 4
ITERS = 4
LANES = 128

viscous_step = 0.5
time_step = 0.02
relaxation = 0.8
f32 = jnp.float32
bf16 = jnp.bfloat16
MODES = 64
KZ = 128
highest_precision = lax.Precision.HIGHEST


def chebyshev_matrix():
    node_points = np.cos(np.pi * np.arange(8) / 7.0)
    weights = np.where((np.arange(8) == 0) | (np.arange(8) == 7), 2.0, 1.0)
    parity = np.where((np.arange(8)[:, None] + np.arange(8)[None, :]) % 2 == 0, 1.0, -1.0)
    identity = np.eye(8)
    spacing = node_points[:, None] - node_points[None, :] + identity
    off_diagonal = weights[:, None] / weights[None, :] * parity / spacing * (1.0 - identity)
    return off_diagonal - identity * off_diagonal.sum(axis=1)[:, None]


def pair(table):
    table = np.asarray(table, np.float32)
    high = table.astype(bf16)
    low = (table - high.astype(np.float32)).astype(bf16)
    return high, low


def spanwise_tables(modes):
    angle = 2.0 * math.pi / NZ * (np.arange(NZ)[:, None] * np.arange(modes)[None, :] % NZ)
    rate = 4.0 * np.arange(modes) / modes
    cosine, sine = np.cos(angle), np.sin(angle)
    basis = np.concatenate([cosine, sine], axis=1)
    slope = np.concatenate([-rate * sine, rate * cosine], axis=1)
    factor = np.full(2 * modes, 2.0 / NZ)
    factor[0] = 1.0 / NZ
    forward = basis.T * factor[:, None]

    def left_three(table):
        high, low = pair(table)
        return np.concatenate([high, low, high], axis=1)

    return left_three(basis), left_three(slope), np.stack(pair(forward))


def plane_tables():
    chebyshev = chebyshev_matrix()
    position = np.arange(LANES)
    column, row, element = position % 8, position // 8 % 8, position // 64
    same = element[:, None] == element[None, :]
    xi = np.where(same & (row[:, None] == row[None, :]), chebyshev.T[column][:, column], 0.0)
    eta = np.where(same & (column[:, None] == column[None, :]), chebyshev.T[row][:, row], 0.0)
    return np.stack(pair(np.concatenate([xi, eta], axis=1)))


def row_order(modes):
    move = np.zeros((modes * 8, 6 * modes), np.float32)
    for field in range(6):
        for mode in range(modes):
            move[mode * 8 + field, field * modes + mode] = 1.0
    shuffle = np.zeros((6 * modes, 6 * modes), np.float32)
    for c in range(3):
        for half in range(2):
            for mode in range(modes):
                shuffle[(2 * c + half) * modes + mode, (c * modes + mode) * 2 + half] = 1.0
    return [table.astype(bf16) for table in (move, move.T, shuffle, shuffle.T @ move.T)]


def dot(a, b):
    return lax.dot_general(a, b, (((1,), (0,)), ((), ())), preferred_element_type=f32)


def split(value):
    high = value.astype(bf16)
    return high, (value - high.astype(f32)).astype(bf16)


def both(value):
    high = value.astype(bf16).astype(f32)
    low = value - high
    tiles = []
    for start in range(0, value.shape[0], 8):
        tiles += [high[start : start + 8], low[start : start + 8]]
    return jnp.concatenate(tiles, axis=0).astype(bf16)


def folded(value):
    tiles = [
        value[start : start + 8] + value[start + 8 : start + 16]
        for start in range(0, value.shape[0], 16)
    ]
    return jnp.concatenate(tiles, axis=0)


def product(value, high, low):
    parts = both(value)
    return folded(dot(parts, high) + dot(parts, low))


def moved(value, one_hot):
    return folded(dot(both(value), one_hot))


def reordered(move, value):
    high, low = split(value)
    return dot(move, high) + dot(move, low)


def exactly(move, value):
    high, low = split(value)
    rest = (value - high.astype(f32) - low.astype(f32)).astype(bf16)
    return dot(move, high) + (dot(move, low) + dot(move, rest))


def kernel(
    ranks,
    depth,
    modes,
    patches,
    width,
    trace,
    share,
    velocity,
    metric_main,
    metric_cross,
    stiffness,
    mass,
    trace_map,
    tables,
    forward,
    plane,
    move,
    back,
    enter,
    leave,
    precond,
    out,
    raw,
    inverse_high,
    inverse_low,
    stiff_high,
    stiff_low,
    across,
    edge_high,
    edge_low,
    beyond_high,
    beyond_low,
    rows_high,
    rows_low,
    gate_high,
    gate_low,
    pick,
    pick_back,
    corner_out,
    corner_in,
    corner_high,
    corner_low,
    state,
    coef,
    hat,
    returned,
    local,
    damped,
    weight,
    iterate,
    note_out,
    note_in,
    raw_sem,
    own_sem,
    coef_send,
    hat_send,
    coef_sem,
    hat_sem,
    note_send,
    note_recv,
    corner_send,
    corner_recv,
):
    me = lax.axis_index("mode")
    place = lax.axis_index("elem")
    has = (place > 0, place < depth - 1)
    beside = (place - 1, place + 1)
    rows = 8 * modes
    wide = modes * trace

    def patch_of(p):
        return pl.ds(p * width, width)

    for k in range(modes):
        for p in range(patches):
            pltpu.make_async_copy(
                precond.at[k, patch_of(p), :], raw.at[k, patch_of(p), :], raw_sem.at[k, p]
            ).start()

    note_in[...] = jnp.zeros_like(note_in)
    corner_in[...] = jnp.zeros_like(corner_in)
    state[...] = exactly(enter[...], velocity[...].reshape(6 * modes, patches * width)).reshape(
        6, modes, patches * width
    )

    barrier = pltpu.get_barrier_semaphore()
    for offset in range(1, ranks):
        pl.semaphore_signal(
            barrier, 1, device_id={"mode": lax.rem(me + offset, ranks)},
            device_id_type=pl.DeviceIdType.MESH,
        )
    for side in range(2):
        @pl.when(has[side])
        def _():
            pl.semaphore_signal(
                barrier, 1, device_id={"elem": beside[side]}, device_id_type=pl.DeviceIdType.MESH
            )
    near_side = (jnp.minimum(place, 1), jnp.minimum(depth - 1 - place, 1))
    near_count = [side.astype(f32) for side in near_side]
    pl.semaphore_wait(barrier, ranks - 1 + near_side[0] + near_side[1])

    def points_of(rank):
        return pl.ds(pl.multiple_of(rank * share, share), share)

    def modes_of(rank):
        return pl.ds(pl.multiple_of(rank * modes, modes), modes)

    def coef_copy(offset):
        to = lax.rem(me + offset, ranks)
        return pltpu.make_async_remote_copy(
            src_ref=state.at[:, :, points_of(to)],
            dst_ref=coef.at[:, modes_of(me), :],
            send_sem=coef_send.at[offset],
            recv_sem=coef_sem.at[offset],
            device_id={"mode": to},
            device_id_type=pl.DeviceIdType.MESH,
        )

    def hat_copy(offset, c):
        to = lax.rem(me + offset, ranks)
        return pltpu.make_async_remote_copy(
            src_ref=hat.at[pl.ds(2 * c, 2), modes_of(to), :],
            dst_ref=returned.at[pl.ds(2 * c, 2), :, points_of(me)],
            send_sem=hat_send.at[c, offset],
            recv_sem=hat_sem.at[c, offset],
            device_id={"mode": to},
            device_id_type=pl.DeviceIdType.MESH,
        )

    def own_coef():
        return pltpu.make_async_copy(
            state.at[:, :, points_of(me)], coef.at[:, modes_of(me), :], own_sem.at[0]
        )

    def own_hat():
        return pltpu.make_async_copy(
            hat.at[:, modes_of(me), :], returned.at[:, :, points_of(me)], own_sem.at[1]
        )

    def send_coef():
        for offset in range(1, ranks):
            coef_copy(offset).start()
        own_coef().start()

    def note_copy(side, slot):
        return pltpu.make_async_remote_copy(
            src_ref=note_out.at[side],
            dst_ref=note_in.at[slot, 1 - side],
            send_sem=note_send.at[side],
            recv_sem=note_recv.at[slot, 1 - side],
            device_id={"elem": beside[side]},
            device_id_type=pl.DeviceIdType.MESH,
        )

    def corner_copy(side):
        return pltpu.make_async_remote_copy(
            src_ref=corner_out.at[side],
            dst_ref=corner_in.at[1 - side],
            send_sem=corner_send.at[side],
            recv_sem=corner_recv.at[1 - side],
            device_id={"elem": beside[side]},
            device_id_type=pl.DeviceIdType.MESH,
        )

    def note_wait(side, slot):
        note_copy(side, slot).wait_send()
        pltpu.make_async_remote_copy(
            src_ref=note_out.at[side],
            dst_ref=note_in.at[slot, side],
            send_sem=note_send.at[side],
            recv_sem=note_recv.at[slot, side],
            device_id={"elem": beside[side]},
            device_id_type=pl.DeviceIdType.MESH,
        ).wait_recv()

    def corner_wait(side):
        corner_copy(side).wait_send()
        pltpu.make_async_remote_copy(
            src_ref=corner_out.at[side],
            dst_ref=corner_in.at[side],
            send_sem=corner_send.at[side],
            recv_sem=corner_recv.at[side],
            device_id={"elem": beside[side]},
            device_id_type=pl.DeviceIdType.MESH,
        ).wait_recv()

    send_coef()

    edge_patch = (0, patches - 1)
    point = lax.broadcasted_iota(jnp.int32, (width, LANES), 0)
    for p in range(patches):
        stiff_high[p], stiff_low[p] = split(viscous_step * stiffness[patch_of(p), :])
        multiplicity = jnp.ones((1, width), f32)
        for side in range(2):
            for kind in range(2):
                ahead = jnp.full((1, trace * kind), -1, jnp.int32)
                after = jnp.full((1, LANES - trace * (kind + 1)), -1, jnp.int32)
                points = trace_map[p * 2 + side : p * 2 + side + 1, :]
                slots = jnp.concatenate(([ahead] if kind else []) + [points, after], axis=1)
                one_hot = jnp.where(slots == point, 1.0, 0.0)
                turned = one_hot.T
                pick[p, side, kind] = one_hot.astype(bf16)
                pick_back[p, side, kind] = turned.astype(bf16)
                if kind == 0:
                    gain = near_count[side] if p == edge_patch[side] else 1.0
                    multiplicity += gain * jnp.sum(turned, axis=0, keepdims=True)
        weight[:, patch_of(p)] = relaxation / (multiplicity * multiplicity)
    for p in range(patches - 1):
        across[p, 0] = dot(pick[p, 1, 0], pick_back[p + 1, 0, 0]).astype(bf16)
        across[p, 1] = dot(pick[p + 1, 0, 0], pick_back[p, 1, 0]).astype(bf16)
    number = lax.broadcasted_iota(jnp.int32, (rows, 1), 0) // 8 + me * modes
    rate = 4.0 * number.astype(f32) / (modes * ranks)
    damped[...] = (1.0 + viscous_step * rate * rate) * mass[...]

    def advect_send():
        for offset in range(1, ranks):
            coef_copy(offset).wait_recv()
        own_coef().wait()
        each = 2 * modes * ranks
        fields = coef[...].reshape(3 * each, share)
        high, low = split(fields)
        slopes = dot(high, plane[0]) + dot(low, plane[0]) + dot(high, plane[1])
        xi, eta = slopes[:, :share], slopes[:, share:]
        mine = points_of(me)
        grad_x = metric_main[0:1, mine] * xi + metric_cross[0:1, mine] * eta
        grad_y = metric_cross[1:2, mine] * xi + metric_main[1:2, mine] * eta

        def physical(table, values):
            high, low = split(jnp.concatenate(values, axis=1))
            return dot(table, jnp.concatenate([high, high, low], axis=0))

        def part(value, c):
            return value[c * each : (c + 1) * each]

        plain = physical(tables[...], [part(fields, c) for c in range(3)])
        u, v, w = (plain[:NZ, c * share : (c + 1) * share] for c in range(3))
        for c in range(3):
            slope = physical(tables[:NZ], [part(grad_x, c), part(grad_y, c)])
            advection = (
                u * slope[:, :share]
                + v * slope[:, share:]
                + w * plain[NZ:, c * share : (c + 1) * share]
            )
            high, low = split(advection)
            total = dot(forward[0], high) + dot(forward[0], low) + dot(forward[1], high)
            hat[pl.ds(2 * c, 2)] = total.reshape(2, modes * ranks, share)
            for offset in range(1, ranks):
                hat_copy(offset, c).start()
        own_hat().start()

    advect_send()

    def prepare(k, carry):
        span = pl.ds(pl.multiple_of(k * trace, trace), trace)
        for p in range(patches):
            pltpu.make_async_copy(
                precond.at[k, patch_of(p), :], raw.at[k, patch_of(p), :], raw_sem.at[k, p]
            ).wait()
            block = raw[k, patch_of(p), :]
            high, low = split(block.T)
            inverse_high[k, p] = high
            inverse_low[k, p] = low
            plain_high, plain_low = split(block)
            for side in range(2):
                if p == edge_patch[side]:
                    choose = pick_back[p, side, 0, :trace, :]
                    edge_high[side, span, :] = dot(choose, high).astype(bf16)
                    edge_low[side, span, :] = dot(choose, low).astype(bf16)
                    rows_high[side, span, :] = dot(choose, plain_high)
                    rows_low[side, span, :] = dot(choose, plain_low)
        return carry

    lax.fori_loop(0, modes, prepare, 0)
    for side in range(2):
        choose = pick[edge_patch[side], side, 1]
        corner_out[side] = dot(edge_high[side], choose) + dot(edge_low[side], choose)

        @pl.when(has[side])
        def _():
            corner_copy(side).start()
    for side in range(2):
        gate_high[side, :, :wide] = rows_high[side].T.astype(bf16)
        gate_high[side, :, wide:] = pick[edge_patch[side], side, 0]
        gate_low[side] = rows_low[side].T.astype(bf16)
        inward = across[0 if side == 0 else patches - 2, side]
        beyond_high[side] = dot(edge_high[side], inward).astype(bf16)
        beyond_low[side] = dot(edge_low[side], inward).astype(bf16)
    for side in range(2):
        @pl.when(has[side])
        def _():
            corner_wait(side)
        corner_high[side], corner_low[side] = split(corner_in[side])

    lane = lax.broadcasted_iota(jnp.int32, (rows, LANES), 1)
    block_mask = (
        lax.broadcasted_iota(jnp.int32, (rows, wide), 0) // 8
        == lax.broadcasted_iota(jnp.int32, (rows, wide), 1) // trace
    )

    def packed(note):
        half = rows // 2
        return jnp.where(
            lane[:half] < LANES // 2, note[:half], pltpu.roll(note[half:], LANES // 2, 1)
        )

    def unpacked(note):
        return jnp.concatenate([note, pltpu.roll(note, LANES // 2, 1)], axis=0)

    def repeated(value):
        total = value
        for turn in range(1, LANES // trace):
            total = total + pltpu.roll(value, turn * trace, 1)
        return total

    def spread(note):
        total = repeated(jnp.where(lane < trace, note, 0.0))
        tiled = jnp.concatenate([total] * (wide // LANES), axis=1)
        return jnp.where(block_mask, tiled, 0.0)

    def noted(parts, side):
        sent = folded(dot(parts, gate_high[side]))
        traced = sent[:, :wide] + folded(dot(parts, gate_low[side]))
        traced = jnp.where(block_mask, traced, 0.0)
        total = traced[:, :LANES]
        for start in range(LANES, wide, LANES):
            total = total + traced[:, start : start + LANES]
        return sent[:, wide:] + jnp.where(lane >= trace, repeated(total), 0.0)

    def advect_receive():
        for offset in range(1, ranks):
            coef_copy(offset).wait_send()
            for c in range(3):
                hat_copy(offset, c).wait_recv()
        own_hat().wait()
        for offset in range(1, ranks):
            for c in range(3):
                hat_copy(offset, c).wait_send()
        source = (state[...] - time_step * returned[...]).reshape(6 * modes, patches * width)
        local[...] = mass[...] * reordered(move[...], source)

    def assembled(parts):
        result = list(parts)
        for p in range(patches - 1):
            result[p + 1] = result[p + 1] + moved(parts[p], across[p, 0])
            result[p] = result[p] + moved(parts[p + 1], across[p, 1])
        return result

    def sweep(number, first):
        slot = lax.rem(number, 2)
        terms = []
        for p in range(patches):
            term = local[:, patch_of(p)]
            if not first:
                value = iterate[:, patch_of(p)]
                term = (
                    term
                    - product(value, stiff_high[p], stiff_low[p])
                    - damped[:, patch_of(p)] * value
                )
            terms.append(term)
        lines = [both(term) for term in assembled(terms)]

        def corrected(p, k):
            line = lines[p][k * 16 : (k + 1) * 16]
            return dot(line, inverse_high[k, p]) + dot(line, inverse_low[k, p])

        notes = [noted(lines[edge_patch[side]], side) for side in range(2)]
        for side in range(2):
            note_out[side] = packed(notes[side])
        first_found = [corrected(0, k) for k in range(2)]
        for side in range(2):
            @pl.when(has[side])
            def _():
                note_copy(side, slot).start()
        parts = []
        for p in range(patches):
            found = list(first_found) if p == 0 else []
            found += [corrected(p, k) for k in range(len(found), modes)]
            parts.append(folded(jnp.concatenate(found, axis=0)))
        total = assembled(parts)
        near = [product(spread(notes[side]), corner_high[side], corner_low[side]) for side in range(2)]
        for side in range(2):
            @pl.when(has[side])
            def _():
                note_wait(side, slot)
        gains = [jnp.zeros((rows, width), f32)] * patches
        for side in range(2):
            p, inner = edge_patch[side], edge_patch[side] + 1 - 2 * side
            note = unpacked(note_in[slot, side])
            spread_note = both(spread(note))
            gains[p] = gains[p] + folded(
                dot(spread_note, edge_high[side])
                + dot(spread_note, edge_low[side])
                + dot(both(note + near[side]), pick_back[p, side, 1])
            )
            gains[inner] = gains[inner] + folded(
                dot(spread_note, beyond_high[side]) + dot(spread_note, beyond_low[side])
            )
        for p in range(patches):
            step = weight[:, patch_of(p)] * (total[p] + gains[p])
            iterate[:, patch_of(p)] = step if first else iterate[:, patch_of(p)] + step

    def later_sweep(number, carry):
        sweep(number, False)
        return carry

    def level(number, carry):
        advect_receive()
        sweep(0, True)
        lax.fori_loop(1, ITERS, later_sweep, 0)
        state[...] = reordered(back[...], iterate[...]).reshape(6, modes, patches * width)

        @pl.when(number < STEPS - 1)
        def _():
            send_coef()
            advect_send()

        return carry

    lax.fori_loop(0, STEPS, level, 0)
    out[...] = exactly(leave[...], iterate[...]).reshape(3, 2 * modes, patches * width)


def on_device(velocity, metric_main, metric_cross, stiffness, mass, precond, trace_map):
    ranks, depth = lax.axis_size("mode"), lax.axis_size("elem")
    rows, points = velocity.shape[1:]
    modes = rows // 2
    patches, _, trace = trace_map.shape
    width = stiffness.shape[1]
    share = points // ranks
    if modes % 8 or share != LANES or LANES != 4 * trace or (modes * trace) % LANES or patches < 2:
        return general_device(
            velocity, metric_main, metric_cross, stiffness, mass, precond, trace_map
        )
    basis, slope, forward = spanwise_tables(modes * ranks)
    vmem = pl.BlockSpec(memory_space=pltpu.VMEM)
    wide = modes * trace
    blocks = (modes, patches, width, width)
    return pl.pallas_call(
        functools.partial(kernel, ranks, depth, modes, patches, width, trace, share),
        out_shape=jax.ShapeDtypeStruct(velocity.shape, f32),
        in_specs=[vmem] * 13 + [pl.BlockSpec(memory_space=pl.ANY)],
        out_specs=vmem,
        scratch_shapes=[
            pltpu.VMEM((modes, patches * width, width), f32),
            pltpu.VMEM(blocks, bf16),
            pltpu.VMEM(blocks, bf16),
            pltpu.VMEM((patches, width, width), bf16),
            pltpu.VMEM((patches, width, width), bf16),
            pltpu.VMEM((patches - 1, 2, width, width), bf16),
            pltpu.VMEM((2, wide, width), bf16),
            pltpu.VMEM((2, wide, width), bf16),
            pltpu.VMEM((2, wide, width), bf16),
            pltpu.VMEM((2, wide, width), bf16),
            pltpu.VMEM((2, wide, width), f32),
            pltpu.VMEM((2, wide, width), f32),
            pltpu.VMEM((2, width, wide + LANES), bf16),
            pltpu.VMEM((2, width, wide), bf16),
            pltpu.VMEM((patches, 2, 2, width, LANES), bf16),
            pltpu.VMEM((patches, 2, 2, LANES, width), bf16),
            pltpu.VMEM((2, wide, LANES), f32),
            pltpu.VMEM((2, wide, LANES), f32),
            pltpu.VMEM((2, wide, LANES), bf16),
            pltpu.VMEM((2, wide, LANES), bf16),
            pltpu.VMEM((6, modes, points), f32),
            pltpu.VMEM((6, modes * ranks, share), f32),
            pltpu.VMEM((6, modes * ranks, share), f32),
            pltpu.VMEM((6, modes, points), f32),
            pltpu.VMEM((8 * modes, points), f32),
            pltpu.VMEM((8 * modes, points), f32),
            pltpu.VMEM((1, points), f32),
            pltpu.VMEM((8 * modes, points), f32),
            pltpu.VMEM((2, 4 * modes, LANES), f32),
            pltpu.VMEM((2, 2, 4 * modes, LANES), f32),
            pltpu.SemaphoreType.DMA((modes, patches)),
            pltpu.SemaphoreType.DMA((2,)),
            pltpu.SemaphoreType.DMA((ranks,)),
            pltpu.SemaphoreType.DMA((3, ranks)),
            pltpu.SemaphoreType.DMA((ranks,)),
            pltpu.SemaphoreType.DMA((3, ranks)),
            pltpu.SemaphoreType.DMA((2,)),
            pltpu.SemaphoreType.DMA((2, 2)),
            pltpu.SemaphoreType.DMA((2,)),
            pltpu.SemaphoreType.DMA((2,)),
        ],
        compiler_params=pltpu.CompilerParams(
            collective_id=0, has_side_effects=True, vmem_limit_bytes=56 * 1024 * 1024
        ),
    )(
        velocity,
        metric_main,
        metric_cross,
        stiffness,
        mass.reshape(1, points),
        trace_map.reshape(patches * 2, trace),
        jnp.asarray(np.concatenate([basis, slope], axis=0)),
        jnp.asarray(forward),
        jnp.asarray(plane_tables()),
        *[jnp.asarray(table) for table in row_order(modes)],
        precond,
    )


def shifted(value, axis, steps):
    count = lax.axis_size(axis)
    initial, last = (max(0, -steps), min(count, count - steps))
    return lax.ppermute(value, axis, [(source, source + steps) for source in range(initial, last)])


def general_spanwise():
    spanwise = jnp.arange(NZ, dtype=jnp.int32)
    row_numbers = jnp.arange(KZ, dtype=jnp.int32)
    wavenumber = row_numbers // 2
    product = spanwise[:, None] * wavenumber[None, :] % NZ
    phase_angle = 2.0 * math.pi / NZ * product.astype(jnp.float32)
    is_sine = (row_numbers % 2 == 1)[None, :]
    basis_table = jnp.where(is_sine, jnp.sin(phase_angle), jnp.cos(phase_angle))
    wave_rate = 4.0 * wavenumber.astype(jnp.float32) / MODES
    slope_table = jnp.where(
        is_sine,
        wave_rate[None, :] * jnp.cos(phase_angle),
        -wave_rate[None, :] * jnp.sin(phase_angle),
    )
    norm_factor = jnp.where(row_numbers == 0, 1.0 / NZ, 2.0 / NZ).astype(jnp.float32)
    forward = basis_table.T * norm_factor[:, None]
    return (basis_table, slope_table, forward, wave_rate)


def general_plane(chebyshev):
    position = jnp.arange(128, dtype=jnp.int32)
    node_column = position % 8
    node_row = position // 8 % 8
    element = position // 64
    eight = jnp.arange(8, dtype=jnp.int32)[None, :]
    pick_column = (node_column[:, None] == eight).astype(jnp.float32)
    pick_row = (node_row[:, None] == eight).astype(jnp.float32)
    same_element = element[:, None] == element[None, :]
    along_xi = jnp.dot(
        jnp.dot(pick_column, chebyshev.T, precision=highest_precision),
        pick_column.T,
        precision=highest_precision,
    )
    along_eta = jnp.dot(
        jnp.dot(pick_row, chebyshev.T, precision=highest_precision),
        pick_row.T,
        precision=highest_precision,
    )
    xi_table = jnp.where(same_element & (node_row[:, None] == node_row[None, :]), along_xi, 0.0)
    eta_table = jnp.where(
        same_element & (node_column[:, None] == node_column[None, :]), along_eta, 0.0
    )
    return (xi_table, eta_table)


def plane_slopes(values, xi_table, eta_table, main_part, cross_part):
    flat_values = values.reshape(-1, 128)
    xi_slope = jnp.dot(flat_values, xi_table, precision=highest_precision).reshape(values.shape)
    eta_slope = jnp.dot(flat_values, eta_table, precision=highest_precision).reshape(values.shape)
    grad_x = main_part[0] * xi_slope + cross_part[0] * eta_slope
    grad_y = cross_part[1] * xi_slope + main_part[1] * eta_slope
    return (grad_x, grad_y)


def general_device(velocity, metric_main, metric_cross, stiffness, mass, precond, trace_map):
    rows_dev = velocity.shape[1]
    points = velocity.shape[2]
    patch_dev = trace_map.shape[0]
    width = stiffness.shape[1]
    trace_width = trace_map.shape[2]
    modes_dev = rows_dev // 2
    chebyshev = jnp.asarray(chebyshev_matrix(), jnp.float32)
    xi_table, eta_table = general_plane(chebyshev)
    basis_table, slope_table, forward, wave_all = general_spanwise()
    wave_rows = lax.dynamic_slice_in_dim(wave_all, lax.axis_index("mode") * rows_dev, rows_dev)
    damping = (1.0 + viscous_step * wave_rows * wave_rows)[None, :, None, None]
    patches = stiffness.reshape(patch_dev, width, width)
    inverse = precond.reshape(modes_dev, patch_dev, width, width)
    patch_mass = mass.reshape(patch_dev, width)
    point_numbers = jnp.arange(width, dtype=jnp.int32)[None, None, :]
    left_pick = (trace_map[:, 0][:, :, None] == point_numbers).astype(jnp.float32)
    right_pick = (trace_map[:, 1][:, :, None] == point_numbers).astype(jnp.float32)
    global_patch = lax.axis_index("elem") * patch_dev + jnp.arange(patch_dev)
    last_patch = patch_dev * lax.axis_size("elem") - 1
    left_gain = (global_patch > 0).astype(jnp.float32)[:, None]
    right_gain = (global_patch < last_patch).astype(jnp.float32)[:, None]
    multiplicity = (
        1.0 + left_gain * jnp.sum(left_pick, axis=1) + right_gain * jnp.sum(right_pick, axis=1)
    )
    weight = relaxation / (multiplicity * multiplicity)
    share = points // lax.axis_size("mode")
    main_share = lax.dynamic_slice_in_dim(metric_main, lax.axis_index("mode") * share, share, 1)
    cross_share = lax.dynamic_slice_in_dim(metric_cross, lax.axis_index("mode") * share, share, 1)

    def assemble(values):
        left_values = jnp.einsum("crpl,pjl->crpj", values, left_pick, precision=highest_precision)
        right_values = jnp.einsum("crpl,pjl->crpj", values, right_pick, precision=highest_precision)
        upward = shifted(right_values[:, :, -1].reshape(-1), "elem", 1)
        downward = shifted(left_values[:, :, 0].reshape(-1), "elem", -1)
        from_below = jnp.concatenate(
            [upward.reshape(3, rows_dev, 1, trace_width), right_values[:, :, :-1]], axis=2
        )
        from_above = jnp.concatenate(
            [left_values[:, :, 1:], downward.reshape(3, rows_dev, 1, trace_width)], axis=2
        )
        below_points = jnp.einsum(
            "crpj,pjl->crpl", from_below, left_pick, precision=highest_precision
        )
        above_points = jnp.einsum(
            "crpj,pjl->crpl", from_above, right_pick, precision=highest_precision
        )
        return values + below_points + above_points

    state = velocity
    for time_level in range(STEPS):
        coefficients = lax.all_to_all(state, "mode", split_axis=2, concat_axis=1, tiled=True)
        grad_x, grad_y = plane_slopes(coefficients, xi_table, eta_table, main_share, cross_share)
        plane_part = jnp.einsum(
            "frp,zr->fpz",
            jnp.concatenate([coefficients, grad_x, grad_y], axis=0),
            basis_table,
            precision=highest_precision,
        )
        spanwise_part = jnp.einsum(
            "frp,zr->fpz", coefficients, slope_table, precision=highest_precision
        )
        physical = jnp.concatenate([plane_part, spanwise_part], axis=0)
        advection = (
            physical[0:1] * physical[3:6]
            + physical[1:2] * physical[6:9]
            + physical[2:3] * physical[9:12]
        )
        advection_points = jnp.einsum(
            "ipz,rz->irp", advection, forward, precision=highest_precision
        )
        advection_hat = lax.all_to_all(
            advection_points, "mode", split_axis=1, concat_axis=2, tiled=True
        )
        source = (state - time_step * advection_hat).reshape(3, rows_dev, patch_dev, width)
        local_term = patch_mass * source
        iterate = jnp.zeros_like(source)
        for sweep_number in range(ITERS):
            if sweep_number == 0:
                residual = assemble(local_term)
            else:
                stiff_part = jnp.einsum(
                    "pij,crpj->crpi", patches, iterate, precision=highest_precision
                )
                residual = assemble(
                    local_term - viscous_step * stiff_part - damping * patch_mass * iterate
                )
            grouped = residual.reshape(3, modes_dev, 2, patch_dev, width)
            correction = jnp.einsum(
                "kpij,ckhpj->ckhpi", inverse, grouped, precision=highest_precision
            ).reshape(3, rows_dev, patch_dev, width)
            iterate = iterate + weight * assemble(correction)
        state = iterate.reshape(3, rows_dev, points)
    return state


def solution(mesh):
    return jax.shard_map(
        on_device,
        mesh=mesh,
        in_specs=(
            P(None, "mode", "elem"),
            P(None, "elem"),
            P(None, "elem"),
            P("elem", None),
            P("elem"),
            P("mode", "elem", None),
            P("elem", None, None),
        ),
        out_specs=P(None, "mode", "elem"),
        check_vma=False,
    )
```
